128 devices in a mesh: ha: 16 (over x, y_hi, core), wa: 8 (over y_lo, z).
Axes of the slice: x: 4, y: 4 (y_hi: 2, y_lo: 2; y = y_hi * 2 + y_lo), z: 4, core: 2. Of those that a mesh axis runs over, the one named last changes fastest.
Arguments:
- latent_map: bfloat16 [384, 128, 160], P('wa', 'ha'), may hold values from -6 to 6
- coarse_cache: bfloat16 [2, 384, 128, 160], P(None, 'wa', 'ha'), may hold values from -6 to 6
- coarse_gain: float32 [384], replicated, may hold values from 0.1 to 1.9
- coarse_kernel: bfloat16 [3, 3, 3, 384, 384], replicated, may hold values from -0.0625 to 0.0625
- coarse_bias: float32 [384], replicated, may hold values from -3 to 3
- upper_kernel: bfloat16 [3, 3, 192, 384], replicated, may hold values from -0.109375 to 0.109375
- upper_bias: float32 [192], replicated, may hold values from -3 to 3
- middle_cache: bfloat16 [2, 192, 256, 320], P(None, None, 'ha', 'wa'), may hold values from -6 to 6
- middle_gain: float32 [192], replicated, may hold values from 0.1 to 1.9
- middle_kernel: bfloat16 [3, 3, 3, 384, 192], replicated, may hold values from -0.078125 to 0.078125
- middle_bias: float32 [384], replicated, may hold values from -3 to 3
- bypass_weight: bfloat16 [384, 192], replicated, may hold values from -0.4375 to 0.4375
- bypass_bias: float32 [384], replicated, may hold values from -3 to 3
- finer_kernel: bfloat16 [3, 3, 192, 384], replicated, may hold values from -0.109375 to 0.109375
- finer_bias: float32 [192], replicated, may hold values from -3 to 3
- fine_cache: bfloat16 [2, 192, 512, 640], P(None, None, 'ha', 'wa'), may hold values from -6 to 6
- fine_gain: float32 [192], replicated, may hold values from 0.1 to 1.9
- fine_kernel: bfloat16 [3, 3, 3, 192, 192], replicated, may hold values from -0.078125 to 0.078125
- fine_bias: float32 [192], replicated, may hold values from -3 to 3
Outputs:
- fine_map: bfloat16 [192, 512, 640], P(None, 'ha', 'wa')
The draws below stay inside these ranges and needn't reach their ends.
All inputs are finite; a program needn't handle non-finite values.
Results may differ from the reference program's by a relative error of at most 0.0095.
Values may be sent and summed in bfloat16 or wider, within the bound.
A program may use at most 320 MiB of HBM per device.

```python
import jax
import jax.numpy as jnp
from jax import lax

CH_HIGH = 384
CH_LOW = 192
LAT_W = 160
LAT_H = 128
MID_H = 256
MID_W = 320
FINE_H = 512
FINE_W = 640


def levels(own_key, extent, cuts, low, largest):
    loudness = 1.0
    for position, parts in cuts:
        heights = jax.random.uniform(jax.random.fold_in(jax.random.fold_in(own_key, 6), position), (parts,), jnp.float32, low / len(cuts), largest / len(cuts))
        loudness = loudness * jnp.repeat(jnp.exp(heights), extent[position] // parts).reshape((-1,) + (1,) * (len(extent) - 1 - position))
    return loudness


def bell_draw(key, dims, scale, bound, split=(), dtype=jnp.bfloat16):
    drawn = jax.random.normal(key, dims, jnp.float32) * scale
    if len(split) > 0:
        drawn = levels(key, dims, split, -0.22, 0.18) * drawn
    return jnp.clip(drawn, min=-bound, max=bound).astype(dtype)


def setup_inputs(seed: int = 0) -> dict:
    streams_of = jax.random.split(jax.random.key(seed), 20)
    return {
        "latent_map": bell_draw(streams_of[0], (CH_HIGH, LAT_H, LAT_W), 1.0, 6.0, ((0, 8), (1, 16))),
        "coarse_cache": bell_draw(streams_of[1], (2, CH_HIGH, LAT_H, LAT_W), 1.0, 6.0, ((1, 8), (2, 16))),
        "coarse_gain": jnp.clip(1.0 + 0.18 * jax.random.normal(streams_of[2], (CH_HIGH,), jnp.float32), 0.1, 1.9),
        "coarse_kernel": bell_draw(streams_of[3], (3, 3, 3, CH_HIGH, CH_HIGH), (27 * CH_HIGH) ** -0.5, 0.0625),
        "coarse_bias": bell_draw(streams_of[4], (CH_HIGH,), 0.5, 3.0, (), jnp.float32),
        "upper_kernel": bell_draw(streams_of[5], (3, 3, CH_LOW, CH_HIGH), (9 * CH_HIGH) ** -0.5, 0.109375),
        "upper_bias": bell_draw(streams_of[6], (CH_LOW,), 0.5, 3.0, (), jnp.float32),
        "middle_cache": bell_draw(streams_of[7], (2, CH_LOW, MID_H, MID_W), 1.0, 6.0, ((2, 16), (3, 8))),
        "middle_gain": jnp.clip(1.0 + 0.18 * jax.random.normal(streams_of[8], (CH_LOW,), jnp.float32), 0.1, 1.9),
        "middle_kernel": bell_draw(streams_of[9], (3, 3, 3, CH_HIGH, CH_LOW), (27 * CH_LOW) ** -0.5, 0.078125),
        "middle_bias": bell_draw(streams_of[10], (CH_HIGH,), 0.5, 3.0, (), jnp.float32),
        "bypass_weight": bell_draw(streams_of[11], (CH_HIGH, CH_LOW), CH_LOW ** -0.5, 0.4375),
        "bypass_bias": bell_draw(streams_of[12], (CH_HIGH,), 0.5, 3.0, (), jnp.float32),
        "finer_kernel": bell_draw(streams_of[13], (3, 3, CH_LOW, CH_HIGH), (9 * CH_HIGH) ** -0.5, 0.109375),
        "finer_bias": bell_draw(streams_of[14], (CH_LOW,), 0.5, 3.0, (), jnp.float32),
        "fine_cache": bell_draw(streams_of[15], (2, CH_LOW, FINE_H, FINE_W), 1.0, 6.0, ((2, 16), (3, 8))),
        "fine_gain": jnp.clip(1.0 + 0.18 * jax.random.normal(streams_of[16], (CH_LOW,), jnp.float32), 0.1, 1.9),
        "fine_kernel": bell_draw(streams_of[17], (3, 3, 3, CH_LOW, CH_LOW), (27 * CH_LOW) ** -0.5, 0.078125),
        "fine_bias": bell_draw(streams_of[18], (CH_LOW,), 0.5, 3.0, (), jnp.float32),
    }


def activate(values, gain):
    wide = values.astype(jnp.float32)
    meansq = lax.optimization_barrier(jnp.mean(wide * wide, axis=0, keepdims=True))
    return jax.nn.silu(wide * lax.rsqrt(meansq + 1e-06) * gain[:, None, None]).astype(jnp.bfloat16)

def enlarge(values):
    return jnp.repeat(jnp.repeat(values, 2, axis=1), 2, axis=2)

def convolve(frames, kernel):
    padded = jnp.pad(frames, ((0, 0), (0, 0), (1, 1), (1, 1))).astype(jnp.float32)
    height = frames.shape[2]
    width = frames.shape[3]
    total = jnp.zeros((kernel.shape[3], height, width), jnp.float32)
    for frame_index in range(kernel.shape[0]):
        for row_tap in range(3):
            for col_tap in range(3):
                piece = padded[frame_index, :, row_tap:row_tap + height, col_tap:col_tap + width]
                weights = kernel[frame_index, row_tap, col_tap].astype(jnp.float32)
                total = total + jnp.einsum('oi,irw->orw', weights, piece, precision=lax.Precision.HIGHEST)
    return total

def reference(latent_map, coarse_cache, coarse_gain, coarse_kernel, coarse_bias, upper_kernel, upper_bias, middle_cache, middle_gain, middle_kernel, middle_bias, bypass_weight, bypass_bias, finer_kernel, finer_bias, fine_cache, fine_gain, fine_kernel, fine_bias):
    act_coarse = activate(latent_map, coarse_gain)
    stacked = jnp.concatenate([coarse_cache, act_coarse[None]], 0)
    coarse = (latent_map.astype(jnp.float32) + convolve(stacked, coarse_kernel) + coarse_bias[:, None, None]).astype(jnp.bfloat16)
    up_mid = (convolve(enlarge(coarse)[None], upper_kernel[None]) + upper_bias[:, None, None]).astype(jnp.bfloat16)
    act_mid = activate(up_mid, middle_gain)
    stacked = jnp.concatenate([middle_cache, act_mid[None]], 0)
    bypass = jnp.einsum('oi,irw->orw', bypass_weight.astype(jnp.float32), up_mid.astype(jnp.float32), precision=lax.Precision.HIGHEST)
    middle = (bypass + bypass_bias[:, None, None] + convolve(stacked, middle_kernel) + middle_bias[:, None, None]).astype(jnp.bfloat16)
    up_fine = (convolve(enlarge(middle)[None], finer_kernel[None]) + finer_bias[:, None, None]).astype(jnp.bfloat16)
    act_fine = activate(up_fine, fine_gain)
    stacked = jnp.concatenate([fine_cache, act_fine[None]], 0)
    fine_map = (up_fine.astype(jnp.float32) + convolve(stacked, fine_kernel) + fine_bias[:, None, None]).astype(jnp.bfloat16)
    return fine_map
```

```python
import functools

import jax
import jax.numpy as jnp
from jax import lax
from jax.experimental import pallas as pl
from jax.experimental.pallas import tpu as pltpu
from jax.sharding import PartitionSpec as P

BF = jnp.bfloat16
F32 = jnp.float32
MESH = pl.DeviceIdType.MESH
NA, NW = 16, 8
EPS = 1e-06
NT = (((1,), (1,)), ((), ()))


def exchange_kernel(pack, ft, mt, edge, coarse, frow, mrow, gedge, send, recv, local):
    a = lax.axis_index("ha")
    w = lax.axis_index("wa")
    north, south = a > 0, a < NA - 1
    west, east = w > 0, w < NW - 1
    barrier = pltpu.get_barrier_semaphore()

    def greet(da, k):
        pl.semaphore_signal(
            barrier, inc=1, device_id=(a + da, lax.rem(w + k, NW)), device_id_type=MESH
        )

    for k in range(1, NW):
        greet(0, k)

    @pl.when(north)
    def _():
        for k in range(NW):
            greet(-1, k)

    @pl.when(south)
    def _():
        for k in range(NW):
            greet(1, k)

    pl.semaphore_wait(barrier, NW - 1 + NW * (jnp.where(north, 1, 0) + jnp.where(south, 1, 0)))

    rows = pl.ds(pl.multiple_of(w * 48, 16), 48)
    copies = []
    slot = [0]

    def remote(src, dst, da, to_w, cond_send, cond_recv):
        s = slot[0]
        slot[0] += 1
        c = pltpu.make_async_remote_copy(
            src_ref=src, dst_ref=dst, send_sem=send.at[s], recv_sem=recv.at[s],
            device_id=(a + da, to_w), device_id_type=MESH)
        copies.append((c, cond_send, cond_recv))

    for k in range(1, NW):
        to = lax.rem(w + k, NW)
        remote(pack.at[to], coarse.at[:, rows, pl.ds(128, 256)], 0, to, None, None)
    for k in range(NW):
        to = lax.rem(w + k, NW)
        remote(pack.at[to, :, :, pl.ds(128, 128)], coarse.at[:, rows, pl.ds(0, 128)], 1, to, south, north)
        remote(pack.at[to, :, :, pl.ds(0, 128)], coarse.at[:, rows, pl.ds(384, 128)], -1, to, north, south)
    remote(ft.at[:, 31], frow.at[0], 1, w, south, north)
    remote(ft.at[:, 0], frow.at[1], -1, w, north, south)
    remote(mt.at[:, pl.ds(14, 2)], mrow.at[0], 1, w, south, north)
    remote(mt.at[:, pl.ds(0, 2)], mrow.at[1], -1, w, north, south)
    remote(edge.at[:, pl.ds(0, 64)], gedge.at[:, pl.ds(0, 64)], 0, w + 1, east, west)
    remote(edge.at[:, pl.ds(64, 64)], gedge.at[:, pl.ds(64, 64)], 0, w - 1, west, east)
    for i, (da, dw) in enumerate(((1, 1), (1, -1), (-1, 1), (-1, -1))):
        go_a, from_a = (south, north) if da == 1 else (north, south)
        go_w, from_w = (east, west) if dw == 1 else (west, east)
        strip = pl.ds(128 + 16 * i, 16)
        remote(edge.at[:, strip], gedge.at[:, strip], da, w + dw,
               jnp.logical_and(go_a, go_w), jnp.logical_and(from_a, from_w))
    for c, cs, _ in copies:
        if cs is None:
            c.start()
        else:
            pl.when(cs)(c.start)
    own = pltpu.make_async_copy(pack.at[w], coarse.at[:, rows, pl.ds(128, 256)], local)
    own.start()
    own.wait()
    for c, cs, cr in copies:
        if cs is None:
            c.wait_send()
            c.wait_recv()
        else:
            pl.when(cs)(c.wait_send)
            pl.when(cr)(c.wait_recv)


def exchange(pack, ft, mt, edge):
    n = 7 + 16 + 10
    return pl.pallas_call(
        exchange_kernel,
        out_shape=(
            jax.ShapeDtypeStruct((3, 384, 512), BF),
            jax.ShapeDtypeStruct((2, 2, 80, 192), BF),
            jax.ShapeDtypeStruct((2, 2, 2, 48, 192), BF),
            jax.ShapeDtypeStruct((2, 192, 192), BF),
        ),
        in_specs=[pl.BlockSpec(memory_space=pl.ANY)] * 4,
        out_specs=[pl.BlockSpec(memory_space=pl.ANY)] * 4,
        scratch_shapes=[
            pltpu.SemaphoreType.DMA((n,)),
            pltpu.SemaphoreType.DMA((n,)),
            pltpu.SemaphoreType.DMA,
        ],
        compiler_params=pltpu.CompilerParams(collective_id=0, has_side_effects=True),
    )(pack, ft, mt, edge)


def act(v, g, channels):
    ms = jnp.sum(v * v, axis=1, keepdims=True) * (1.0 / channels)
    u = v * lax.rsqrt(ms + EPS) * g
    return 0.5 * u * (1.0 + jnp.tanh(0.5 * u))


def nt_dot(x, w):
    return lax.dot_general(x, w, NT, preferred_element_type=F32)


def pack_weights(raw, out):
    n = out.shape[0]
    for a in range(3):
        base = a * 1792

        def half(t, b):
            return raw[t, a, b, :, 128:192]

        for t in range(2):
            for b in range(3):
                out[:, base + (t * 3 + b) * 128 : base + (t * 3 + b + 1) * 128] = raw[t, a, b, :, 0:128]
        pairs = [((0, 0), (0, 1)), ((0, 2), (1, 0)), ((1, 1), (1, 2))]
        for i, (p, q) in enumerate(pairs):
            out[:, base + 768 + i * 128 : base + 896 + i * 128] = jnp.concatenate([half(*p), half(*q)], 1)
        for b in range(3):
            out[:, base + 1152 + b * 128 : base + 1280 + b * 128] = raw[2, a, b, :, 0:128]
        out[:, base + 1536 : base + 1664] = jnp.concatenate([half(2, 0), half(2, 1)], 1)
        out[:, base + 1664 : base + 1792] = jnp.concatenate([half(2, 2), jnp.zeros((n, 64), BF)], 1)


def fold_weights(raw, out):
    def chunk(src, first, step):
        k = [[raw[a, b, pl.ds(src, 16), :].astype(F32) for b in range(3)] for a in range(3)]
        rowed = [[[k[0][b] + k[1][b] for b in range(3)], k[2]],
                 [k[0], [k[1][b] + k[2][b] for b in range(3)]]]
        for sr in range(2):
            for sc in range(2):
                at = pl.multiple_of(first + (sr * 2 + sc) * step, 16)
                for ta in range(2):
                    r = rowed[sr][ta]
                    cols = [r[0] + r[1], r[2]] if sc == 0 else [r[0], r[1] + r[2]]
                    for tb in range(2):
                        lane = (ta * 2 + tb) * 384
                        out[pl.ds(at, 16), lane : lane + 384] = cols[tb].astype(BF)

    def low(c, _):
        chunk(pl.multiple_of(c * 16, 16), c * 16, 128)
        return 0

    def high(c, _):
        chunk(pl.multiple_of(128 + c * 16, 16), 512 + c * 16, 64)
        return 0

    lax.fori_loop(0, 8, low, 0)
    lax.fori_loop(0, 4, high, 0)


def put_phases(block, bias, img, row, first):
    n = block.shape[0]
    lo, hi = bias[:, 0:128], bias[:, 128:192]
    for s in range(4):
        at = pl.ds(first + s % 2, n, stride=2)
        img[0, row + s // 2, at, :] = block[:, s * 128 : s * 128 + 128] + lo
        high = block[:, 512 + s * 64 : 576 + s * 64] + hi
        img[1, row + s // 2, at, :] = jnp.concatenate([high, jnp.zeros((n, 64), F32)], 1)


def image_row(img, row, cols):
    return jnp.concatenate([img[0, row, cols, :], img[1, row, cols, 0:64]], -1)


def put_cached(x, at, n, buf, first):
    v = [[buf[t, first + b : first + b + n, :].astype(BF) for b in range(3)] for t in range(2)]
    rows = pl.ds(at, n)
    for t in range(2):
        for b in range(3):
            x[rows, (t * 3 + b) * 128 : (t * 3 + b + 1) * 128] = v[t][b][:, 0:128]
    pairs = [((0, 0), (0, 1)), ((0, 2), (1, 0)), ((1, 1), (1, 2))]
    for i, (p, q) in enumerate(pairs):
        x[rows, 768 + i * 128 : 896 + i * 128] = jnp.concatenate(
            [v[p[0]][p[1]][:, 128:192], v[q[0]][q[1]][:, 128:192]], 1)


def put_current(x, at, n, buf, first):
    v = [buf[first + b : first + b + n, :].astype(BF) for b in range(3)]
    rows = pl.ds(at, n)
    for b in range(3):
        x[rows, 1152 + b * 128 : 1280 + b * 128] = v[b][:, 0:128]
    x[rows, 1536:1664] = jnp.concatenate([v[0][:, 128:192], v[1][:, 128:192]], 1)
    x[rows, 1664:1792] = jnp.concatenate([v[2][:, 128:192], jnp.zeros((n, 64), BF)], 1)


def compute_kernel(
    coarse, frow, mrow, gedge, ft, mt, ck, uk, mk, bk, nk, fk,
    cgain, cbias, ubias, mgain, mbias, nbias, fgain, fbias,
    out,
    v_coarse, v_f, v_m, v_g, v_ck, v_uk, v_mk, v_bk, v_nk, v_fk,
    wm, wf, w4u, w4n, xf, xm, xb, xu1, xu2,
    img_c, img_l, img1, img_m, img2, img_f, rb_f, rb_m, rb_1, g32,
    lf, rf, lm, rm, ob, sem, osem,
):
    a = lax.axis_index("ha")
    w = lax.axis_index("wa")
    count = [0]

    def load(src, dst):
        c = pltpu.make_async_copy(src, dst, sem.at[count[0]])
        count[0] += 1
        c.start()
        return c

    d_coarse = load(coarse, v_coarse)
    d_ck = [load(ck.at[t], v_ck.at[t]) for t in range(3)]
    d_uk = load(uk, v_uk)
    d_g = load(gedge, v_g)
    d_m = [load(mt, v_m.at[:, pl.ds(2, 16)]), load(mrow.at[0], v_m.at[:, pl.ds(0, 2)]),
           load(mrow.at[1], v_m.at[:, pl.ds(18, 2)])]
    d_mk = load(mk, v_mk)
    d_bk = load(bk, v_bk)
    d_nk = load(nk, v_nk)
    d_f = [load(ft, v_f.at[:, pl.ds(1, 32)]), load(frow.at[0], v_f.at[:, 0]),
           load(frow.at[1], v_f.at[:, 33])]
    d_fk = load(fk, v_fk)

    img1[...] = jnp.zeros_like(img1)
    rb_m[...] = jnp.zeros_like(rb_m)
    rb_1[...] = jnp.zeros_like(rb_1)
    img_m[...] = jnp.zeros_like(img_m)

    d_coarse.wait()
    lane = lax.broadcasted_iota(jnp.int32, (1, 512), 1)
    keep = jnp.logical_and(jnp.logical_or(lane >= 128, a > 0), jnp.logical_or(lane < 384, a < NA - 1))
    for t in range(3):
        for p in range(4):
            part = jnp.where(keep[:, p * 128 : p * 128 + 128],
                             v_coarse[t, :, p * 128 : p * 128 + 128].astype(F32), 0.0)
            flat = part.T
            if t == 2:
                img_l[p * 4 : p * 4 + 4] = flat.reshape(4, 32, 384)
                flat = act(flat, cgain[...], 384)
            img_c[p * 4 : p * 4 + 4, 0:32, :] = flat.reshape(4, 32, 384)
        for b in range(3):
            v = img_c[1:15, b : b + 24, :].reshape(336, 384)
            for ra in range(3):
                at = (t * 3 + ra) * 288
                xf[at : at + 288, b * 384 : b * 384 + 384] = v[ra * 24 : ra * 24 + 288].astype(BF)
    total = img_l[2:14, 1:25, :].reshape(288, 384) + cbias[...]
    for t in range(3):
        d_ck[t].wait()
        x = jnp.concatenate([xf[(t * 3 + ra) * 288 : (t * 3 + ra + 1) * 288, 0:1152] for ra in range(3)], 1)
        k = jnp.concatenate([v_ck[t, ra, b] for ra in range(3) for b in range(3)], 1)
        total = total + nt_dot(x, k)
    rid = lax.broadcasted_iota(jnp.int32, (12, 24, 1), 0) + (a * 8 - 2)
    cid = lax.broadcasted_iota(jnp.int32, (12, 24, 1), 1) + (w * 20 - 2)
    inside = (rid >= 0) & (rid < 128) & (cid >= 0) & (cid < 160)
    img1[:, 0:24, :] = jnp.where(inside, total.reshape(12, 24, 384), 0.0)
    for b in range(2):
        xu1[:, b * 384 : b * 384 + 384] = img1[:, b : b + 32, :].reshape(384, 384).astype(BF)

    d_uk.wait()
    fold_weights(v_uk, w4u)
    x = jnp.concatenate([xu1[0:352, :], xu1[32:384, :]], 1)
    u = nt_dot(x, w4u[...])
    for i in range(11):
        put_phases(u[i * 32 : i * 32 + 32, :], ubias[...], img_m, 2 * i, 5)

    d_g.wait()
    no_n, no_s, no_w, no_e = a == 0, a == NA - 1, w == 0, w == NW - 1
    spans = ((0, 64, no_w), (64, 128, no_e), (128, 144, no_n | no_w), (144, 160, no_n | no_e),
             (160, 176, no_s | no_w), (176, 192, no_s | no_e))
    for lo, hi, gone in spans:
        g32[:, lo:hi, :] = jnp.where(gone, 0.0, v_g[:, lo:hi, :].astype(F32))
    for t in range(2):
        for l, m, base, n, s in ((lf, lm, 0, 128, 160), (rf, rm, 64, 144, 176)):
            l[t, 0:1, :] = g32[t, n : n + 1, :]
            l[t, 1:33, :] = g32[t, base : base + 32, :]
            l[t, 33:34, :] = g32[t, s : s + 1, :]
            m[t, 0:4, :] = g32[t, n + 1 : n + 5, :]
            m[t, 4:36, :] = g32[t, base + 32 : base + 64, :]
            m[t, 36:40, :] = g32[t, s + 1 : s + 5, :]

    for d in d_m:
        d.wait()

    @pl.when(no_n)
    def _():
        v_m[:, 0:2] = jnp.zeros((2, 2, 48, 192), BF)

    @pl.when(no_s)
    def _():
        v_m[:, 18:20] = jnp.zeros((2, 2, 48, 192), BF)

    mcol = lax.broadcasted_iota(jnp.int32, (72, 1), 0) + (w * 40 - 8)
    mcol = jnp.where((mcol >= 0) & (mcol < 320), 1.0, 0.0)

    def mid_row(r, _):
        for t in range(2):
            rb_m[t, 8:48, :] = v_m[t, r, 0:40, :].astype(F32)
            for c in range(2):
                rb_m[t, 6 + c : 7 + c, :] = lm[t, pl.ds(2 * r + c, 1), :]
                rb_m[t, 48 + c : 49 + c, :] = rm[t, pl.ds(2 * r + c, 1), :]
        at = pl.multiple_of(r * 48, 16)
        put_cached(xm, at, 48, rb_m, 6)
        row = a * 16 - 2 + r
        ok = jnp.where((row >= 0) & (row < 256), 1.0, 0.0)
        rb_1[0:72, :] = act(image_row(img_m, r + 1, slice(0, 72)), mgain[...], 192) * (mcol * ok)
        put_current(xm, at, 48, rb_1, 6)
        return 0

    lax.fori_loop(0, 20, mid_row, 0)

    def bypass_row(r, _):
        xb[pl.ds(pl.multiple_of(r * 48, 16), 48), :] = image_row(img_m, r + 2, slice(7, 55)).astype(BF)
        return 0

    lax.fori_loop(0, 18, bypass_row, 0)
    d_mk.wait()
    d_bk.wait()
    pack_weights(v_mk, wm)

    def mid_block(i, _):
        at = pl.multiple_of(i * 288, 16)
        total = nt_dot(xb[pl.ds(at, 288), :], v_bk[...]) + mbias[...]
        for ra in range(3):
            total = total + nt_dot(xm[pl.ds(pl.multiple_of(at + ra * 48, 16), 288), :],
                                   wm[:, ra * 1792 : ra * 1792 + 1792])
        rid = lax.broadcasted_iota(jnp.int32, (6, 48, 1), 0) + (a * 16 - 1 + i * 6)
        cid = lax.broadcasted_iota(jnp.int32, (6, 48, 1), 1) + (w * 40 - 1)
        inside = (rid >= 0) & (rid < 256) & (cid >= 0) & (cid < 320)
        img2[pl.ds(i * 6, 6), 0:48, :] = jnp.where(inside, total.reshape(6, 48, 384), 0.0)
        return 0

    lax.fori_loop(0, 3, mid_block, 0)

    def shift_row(r, _):
        at = pl.multiple_of(r * 48, 16)
        for b in range(2):
            xu2[pl.ds(at, 48), b * 384 : b * 384 + 384] = img2[r, b : b + 48, :].astype(BF)
        return 0

    lax.fori_loop(0, 18, shift_row, 0)
    xu2[864:912, :] = jnp.zeros((48, 768), BF)

    d_nk.wait()
    fold_weights(v_nk, w4n)

    def fine_block(i, _):
        at = pl.multiple_of(i * 288, 16)
        x = jnp.concatenate([xu2[pl.ds(at, 288), :], xu2[pl.ds(pl.multiple_of(at + 48, 16), 288), :]], 1)
        u = nt_dot(x, w4n[...])
        for j in range(6):
            put_phases(u[j * 48 : j * 48 + 48, :], nbias[...], img_f, i * 12 + 2 * j, 7)
        return 0

    lax.fori_loop(0, 3, fine_block, 0)

    for d in d_f:
        d.wait()

    @pl.when(no_n)
    def _():
        v_f[:, 0:1] = jnp.zeros((2, 1, 80, 192), BF)

    @pl.when(no_s)
    def _():
        v_f[:, 33:34] = jnp.zeros((2, 1, 80, 192), BF)

    fcol = lax.broadcasted_iota(jnp.int32, (96, 1), 0) + (w * 80 - 8)
    fcol = jnp.where((fcol >= 0) & (fcol < 640), 1.0, 0.0)

    def fine_row(r, _):
        for t in range(2):
            rb_f[t, 8:88, :] = v_f[t, r].astype(F32)
            rb_f[t, 7:8, :] = lf[t, pl.ds(r, 1), :]
            rb_f[t, 88:89, :] = rf[t, pl.ds(r, 1), :]
        at = pl.multiple_of(r * 80, 16)
        put_cached(xf, at, 80, rb_f, 7)
        row = a * 32 - 1 + r
        ok = jnp.where((row >= 0) & (row < 512), 1.0, 0.0)
        rb_1[0:96, :] = act(image_row(img_f, r, slice(0, 96)), fgain[...], 192) * (fcol * ok)
        put_current(xf, at, 80, rb_1, 7)
        return 0

    lax.fori_loop(0, 34, fine_row, 0)
    d_fk.wait()
    pack_weights(v_fk, wf)

    def out_block(i, _):
        at = pl.multiple_of(i * 640, 16)
        total = image_row(img_f, pl.ds(1 + i * 8, 8), slice(8, 88)).reshape(640, 192) + fbias[...]
        for ra in range(3):
            total = total + nt_dot(xf[pl.ds(pl.multiple_of(at + ra * 80, 16), 640), :],
                                   wf[:, ra * 1792 : ra * 1792 + 1792])
        ob[pl.ds(at, 640), :] = total.astype(BF)
        return 0

    lax.fori_loop(0, 4, out_block, 0)
    done = pltpu.make_async_copy(ob, out, osem)
    done.start()
    done.wait()


def compute(*args):
    anywhere = pl.BlockSpec(memory_space=pl.ANY)
    vmem = pl.BlockSpec(memory_space=pltpu.VMEM)
    V = pltpu.VMEM
    return pl.pallas_call(
        compute_kernel,
        out_shape=jax.ShapeDtypeStruct((2560, 192), BF),
        in_specs=[anywhere] * 12 + [vmem] * 8,
        out_specs=anywhere,
        scratch_shapes=[
            V((3, 384, 512), BF), V((2, 34, 80, 192), BF), V((2, 20, 48, 192), BF), V((2, 192, 192), BF),
            V((3, 3, 3, 384, 384), BF), V((3, 3, 192, 384), BF), V((3, 3, 3, 384, 192), BF),
            V((384, 192), BF), V((3, 3, 192, 384), BF), V((3, 3, 3, 192, 192), BF),
            V((384, 5376), BF), V((192, 5376), BF), V((768, 1536), BF), V((768, 1536), BF),
            V((2720, 1792), BF), V((960, 1792), BF), V((864, 192), BF), V((384, 768), BF), V((912, 768), BF),
            V((16, 40, 384), F32), V((16, 32, 384), F32), V((12, 40, 384), F32), V((2, 22, 72, 128), F32),
            V((18, 56, 384), F32), V((2, 36, 104, 128), F32), V((2, 96, 192), F32), V((2, 72, 192), F32),
            V((96, 192), F32), V((2, 192, 192), F32),
            V((2, 40, 192), F32), V((2, 40, 192), F32), V((2, 40, 192), F32), V((2, 40, 192), F32),
            V((2560, 192), BF),
            pltpu.SemaphoreType.DMA((16,)), pltpu.SemaphoreType.DMA,
        ],
        compiler_params=pltpu.CompilerParams(vmem_limit_bytes=62 * 2**20),
    )(*args)


def per_device(
    latent_map, coarse_cache, coarse_gain, coarse_kernel, coarse_bias, upper_kernel, upper_bias,
    middle_cache, middle_gain, middle_kernel, middle_bias, bypass_weight, bypass_bias,
    finer_kernel, finer_bias, fine_cache, fine_gain, fine_kernel, fine_bias,
):
    stacked = jnp.concatenate([coarse_cache, latent_map[None]], 0)
    wide = jnp.pad(stacked, ((0, 0), (0, 0), (0, 0), (3, 9)))
    pack = jnp.stack([wide[:, :, :, 20 * i : 20 * i + 32] for i in range(NW)], 0).reshape(NW, 3, 48, 256)
    ft = jnp.transpose(fine_cache, (0, 2, 3, 1))
    mt = jnp.pad(jnp.transpose(middle_cache, (0, 2, 3, 1)), ((0, 0), (0, 0), (0, 8), (0, 0)))

    def corner(r, c):
        f = fine_cache[:, :, 31 * r : 31 * r + 1, 79 * c : 79 * c + 1].reshape(2, 192, 1)
        m = middle_cache[:, :, 14 * r : 14 * r + 2, 38 * c : 38 * c + 2].reshape(2, 192, 4)
        return jnp.pad(jnp.concatenate([f, m], 2), ((0, 0), (0, 0), (0, 11)))

    def strip(c):
        f = fine_cache[:, :, :, 79 * c]
        m = middle_cache[:, :, :, 38 * c : 38 * c + 2].reshape(2, 192, 32)
        return jnp.concatenate([f, m], 2)

    edge = jnp.concatenate([strip(1), strip(0), corner(1, 1), corner(1, 0), corner(0, 1), corner(0, 0)], 2)
    edge = jnp.transpose(edge, (0, 2, 1))
    coarse, frow, mrow, gedge = exchange(pack, ft, mt, edge)
    row = lambda v: v.reshape(1, -1)
    y = compute(
        coarse, frow, mrow, gedge, ft, mt, coarse_kernel, upper_kernel, middle_kernel, bypass_weight,
        finer_kernel, fine_kernel, row(coarse_gain), row(coarse_bias), row(upper_bias), row(middle_gain),
        row(middle_bias + bypass_bias), row(finer_bias), row(fine_gain), row(fine_bias))
    return jnp.transpose(y.reshape(32, 80, 192), (2, 0, 1))


def solution(mesh):
    high = (P("wa", "ha", None), P(None, "wa", "ha", None))
    low = P(None, None, "ha", "wa")
    placed = high + (P(),) * 5 + (low,) + (P(),) * 7 + (low,) + (P(),) * 3
    return jax.shard_map(
        per_device, mesh=mesh, in_specs=placed, out_specs=P(None, "ha", "wa"), check_vma=False
    )
```

```python
import jax
import jax.numpy as jnp
from jax import lax
from jax.experimental import pallas as pl
from jax.experimental.pallas import tpu as pltpu
from jax.sharding import PartitionSpec as P

BF = jnp.bfloat16
F32 = jnp.float32
MESH = pl.DeviceIdType.MESH
NA, NW = 16, 8
EPS = 1e-06
NT = (((1,), (1,)), ((), ()))


def act(v, g, channels):
    ms = jnp.sum(v * v, axis=1, keepdims=True) * (1.0 / channels)
    u = v * lax.rsqrt(ms + EPS) * g
    return 0.5 * u * (1.0 + jnp.tanh(0.5 * u))


def nt_dot(x, w):
    return lax.dot_general(x, w, NT, preferred_element_type=F32)


def fold_weights(raw, out):
    def chunk(src, first, step):
        k = [[raw[a, b, pl.ds(src, 16), :].astype(F32) for b in range(3)] for a in range(3)]
        rowed = [[[k[0][b] + k[1][b] for b in range(3)], k[2]],
                 [k[0], [k[1][b] + k[2][b] for b in range(3)]]]
        for sr in range(2):
            for sc in range(2):
                at = first + (sr * 2 + sc) * step
                for ta in range(2):
                    r = rowed[sr][ta]
                    cols = [r[0] + r[1], r[2]] if sc == 0 else [r[0], r[1] + r[2]]
                    for tb in range(2):
                        lane = (ta * 2 + tb) * 384
                        out[pl.ds(at, 16), lane : lane + 384] = cols[tb].astype(BF)

    for c in range(8):
        chunk(c * 16, c * 16, 128)
    for c in range(4):
        chunk(128 + c * 16, 512 + c * 16, 64)


def put_phases(block, bias, img, row, first):
    n = block.shape[0]
    lo, hi = bias[:, 0:128], bias[:, 128:192]
    for s in range(4):
        at = pl.ds(first + s % 2, n, stride=2)
        img[0, row + s // 2, at, :] = block[:, s * 128 : s * 128 + 128] + lo
        high = block[:, 512 + s * 64 : 576 + s * 64] + hi
        img[1, row + s // 2, at, :] = jnp.concatenate([high, jnp.zeros((n, 64), F32)], 1)


def image_row(img, row, cols):
    return jnp.concatenate([img[0, row, cols, :], img[1, row, cols, 0:64]], -1)


def pack_fine(raw, cached, current):
    n = cached.shape[0]
    for a in range(3):
        c = a * 1152
        for t in range(2):
            for b in range(3):
                i = t * 3 + b
                cached[:, c + i * 128 : c + i * 128 + 128] = raw[t, a, b, :, 0:128]
        for i in range(3):
            p, q = 2 * i, 2 * i + 1
            cached[:, c + 768 + i * 128 : c + 896 + i * 128] = jnp.concatenate(
                [raw[p // 3, a, p % 3, :, 128:192], raw[q // 3, a, q % 3, :, 128:192]], 1)
        c = a * 640
        for b in range(3):
            current[:, c + b * 128 : c + b * 128 + 128] = raw[2, a, b, :, 0:128]
        current[:, c + 384 : c + 512] = jnp.concatenate([raw[2, a, 0, :, 128:192], raw[2, a, 1, :, 128:192]], 1)
        current[:, c + 512 : c + 640] = jnp.concatenate([raw[2, a, 2, :, 128:192], jnp.zeros((n, 64), BF)], 1)


def put_cached(x, at, n, buf, first):
    v = [buf[i // 3, first + i % 3 : first + i % 3 + n, :].astype(BF) for i in range(6)]
    rows = pl.ds(at, n)
    for i in range(6):
        x[rows, i * 128 : i * 128 + 128] = v[i][:, 0:128]
    for i in range(3):
        x[rows, 768 + i * 128 : 896 + i * 128] = jnp.concatenate(
            [v[2 * i][:, 128:192], v[2 * i + 1][:, 128:192]], 1)


def put_current(x, at, n, buf, first):
    v = [buf[first + b : first + b + n, :].astype(BF) for b in range(3)]
    rows = pl.ds(at, n)
    for b in range(3):
        x[rows, b * 128 : b * 128 + 128] = v[b][:, 0:128]
    x[rows, 384:512] = jnp.concatenate([v[0][:, 128:192], v[1][:, 128:192]], 1)
    x[rows, 512:640] = jnp.concatenate([v[2][:, 128:192], jnp.zeros((n, 64), BF)], 1)


def taps(x, at, n, pitch):
    return jnp.concatenate([x[pl.ds(at + r * pitch, n), :] for r in range(3)], 1)


def kernel(
    lat, cc, g_c, b_c, b_u, g_m, b_m, b_b, b_n, g_f, b_f, ft, mt, ck, uk, mk, bk, nk, fk,
    out,
    v_coarse, v_f, v_m, v_g, v_ck, v_uk, v_mf, v_mh, v_bk, v_nk, v_fk,
    s0, s1, e32, edge, pack, wfc, wf2, w4u, w4n, xfc, xf2, xmc, xm2,
    img_c, img_l, img1, img_m, img2, img_f, rb_f, rb_m, rb_1, g32,
    lf, rf, lm, rm, acc_f, acc_m, sem, osem, send, recv,
):
    a = lax.axis_index("ha")
    w = lax.axis_index("wa")
    north, south = a > 0, a < NA - 1
    west, east = w > 0, w < NW - 1
    barrier = pltpu.get_barrier_semaphore()

    def greet(da, k):
        pl.semaphore_signal(
            barrier, inc=1, device_id=(a + da, lax.rem(w + k, NW)), device_id_type=MESH
        )

    for k in range(1, NW):
        greet(0, k)

    @pl.when(north)
    def _():
        for k in range(NW):
            greet(-1, k)

    @pl.when(south)
    def _():
        for k in range(NW):
            greet(1, k)

    count = [0]

    def load(src, dst):
        c = pltpu.make_async_copy(src, dst, sem.at[count[0]])
        count[0] += 1
        c.start()
        return c

    d_m = load(mt, v_m.at[:, pl.ds(2, 16)])
    d_f = load(ft, v_f.at[:, pl.ds(1, 32)])
    d_uk = load(uk, v_uk)
    d_nk = load(nk, v_nk)
    d_fk = load(fk, v_fk)
    d_mf = load(mk.at[:, :, :, pl.ds(0, 128), :], v_mf)
    d_mh = load(mk.at[:, :, :, pl.ds(128, 64), :], v_mh)
    d_bk = load(bk, v_bk)
    d_ck = [load(ck.at[t], v_ck.at[t]) for t in range(3)]

    def column(ref, t, first, n, tile, col):
        x = ref[t, first : first + n, tile : tile + 8, :].astype(F32)
        s0[0:n] = x[:, :, 0:128]
        s1[0:n] = jnp.concatenate([x[:, :, 128:192], jnp.zeros((n, 8, 64), F32)], 2)
        return [jnp.concatenate([s0[0:n, c, :], s1[0:n, c, 0:64]], 1) for c in col]

    d_m.wait()
    d_f.wait()
    e32[:, 128:192, :] = jnp.zeros((2, 64, 192), F32)
    for t in range(2):
        for side in range(2):
            (f,) = column(v_f, t, 1, 32, 72 - 72 * side, (7 - 7 * side,))
            m = column(v_m, t, 2, 16, 32 - 32 * side, (6 - 6 * side, 7 - 6 * side))
            e32[t, 64 * side : 64 * side + 32, :] = f
            e32[t, 64 * side + 32 : 64 * side + 48, :] = m[0]
            e32[t, 64 * side + 48 : 64 * side + 64, :] = m[1]
            for north_end in range(2):
                at = 128 + 32 * north_end + 16 * side
                h, r = 31 - 31 * north_end, 14 - 14 * north_end
                e32[t, at : at + 1, :] = f[h : h + 1]
                e32[t, at + 1 : at + 3, :] = m[0][r : r + 2]
                e32[t, at + 3 : at + 5, :] = m[1][r : r + 2]
    edge[...] = e32[...].astype(BF)

    quarter = lax.broadcasted_iota(jnp.int32, (1, 128), 1) // 32
    for t in range(3):
        x = (lat[...] if t == 2 else cc[t]).astype(F32)
        s0[...] = x[:, :, 0:128]
        s1[...] = jnp.concatenate([x[:, :, 128:160], jnp.zeros((48, 8, 96), F32)], 2)
        for half in range(2):
            rows4 = [jnp.concatenate([s0[:, half * 4 + h, :], s1[:, half * 4 + h, :]], 1) for h in range(4)]
            for to in range(NW):
                got = None
                for h in range(4):
                    shift = (half * 128 + h * 32 - (20 * to - 3)) % 256
                    moved = pltpu.roll(rows4[h], shift, 1)[:, half * 128 : half * 128 + 128]
                    got = moved if got is None else jnp.where(quarter == h, moved, got)
                pack[to, t, :, half * 128 : half * 128 + 128] = got.astype(BF)

    pl.semaphore_wait(barrier, NW - 1 + NW * (jnp.where(north, 1, 0) + jnp.where(south, 1, 0)))

    mine = pl.ds(pl.multiple_of(w * 48, 16), 48)
    copies = []

    def remote(src, dst, da, to_w, cond_send, cond_recv):
        s = len(copies)
        c = pltpu.make_async_remote_copy(
            src_ref=src, dst_ref=dst, send_sem=send.at[s], recv_sem=recv.at[s],
            device_id=(a + da, to_w), device_id_type=MESH)
        copies.append((c, cond_send, cond_recv))

    remote(edge.at[:, pl.ds(0, 64)], v_g.at[:, pl.ds(0, 64)], 0, w + 1, east, west)
    remote(edge.at[:, pl.ds(64, 64)], v_g.at[:, pl.ds(64, 64)], 0, w - 1, west, east)
    for i, (da, dw) in enumerate(((1, 1), (1, -1), (-1, 1), (-1, -1))):
        go_a, from_a = (south, north) if da == 1 else (north, south)
        go_w, from_w = (east, west) if dw == 1 else (west, east)
        strip = pl.ds(128 + 16 * i, 16)
        remote(edge.at[:, strip], v_g.at[:, strip], da, w + dw,
               jnp.logical_and(go_a, go_w), jnp.logical_and(from_a, from_w))
    n_edge = len(copies)
    remote(mt.at[:, pl.ds(14, 2)], v_m.at[:, pl.ds(0, 2)], 1, w, south, north)
    remote(mt.at[:, pl.ds(0, 2)], v_m.at[:, pl.ds(18, 2)], -1, w, north, south)
    n_mid = len(copies)
    remote(ft.at[:, 31], v_f.at[:, 0], 1, w, south, north)
    remote(ft.at[:, 0], v_f.at[:, 33], -1, w, north, south)
    n_fine = len(copies)
    for k in range(1, NW):
        to = lax.rem(w + k, NW)
        remote(pack.at[to], v_coarse.at[:, mine, pl.ds(128, 256)], 0, to, None, None)
    for k in range(NW):
        to = lax.rem(w + k, NW)
        remote(pack.at[to, :, :, pl.ds(128, 128)], v_coarse.at[:, mine, pl.ds(0, 128)], 1, to, south, north)
        remote(pack.at[to, :, :, pl.ds(0, 128)], v_coarse.at[:, mine, pl.ds(384, 128)], -1, to, north, south)
    for c, cs, _ in copies:
        if cs is None:
            c.start()
        else:
            pl.when(cs)(c.start)

    def arrived(first, last):
        for c, _, cr in copies[first:last]:
            if cr is None:
                c.wait_recv()
            else:
                pl.when(cr)(c.wait_recv)

    v_coarse[:, mine, 128:384] = pack[w]
    cgain, cbias, ubias, mgain, mbias, bbias, nbias, fgain, fbias = [
        v[...].reshape(1, -1) for v in (g_c, b_c, b_u, g_m, b_m, b_b, b_n, g_f, b_f)]
    mbias = mbias + bbias

    img1[...] = jnp.zeros_like(img1)
    rb_m[...] = jnp.zeros_like(rb_m)
    rb_1[...] = jnp.zeros_like(rb_1)
    img_m[...] = jnp.zeros_like(img_m)

    d_uk.wait()
    d_nk.wait()
    d_fk.wait()
    d_mf.wait()
    d_mh.wait()
    d_bk.wait()

    arrived(0, n_fine)
    no_n, no_s, no_w, no_e = a == 0, a == NA - 1, w == 0, w == NW - 1

    @pl.when(no_n)
    def _():
        v_m[:, 0:2] = jnp.zeros((2, 2, 40, 192), BF)
        v_f[:, 0:1] = jnp.zeros((2, 1, 80, 192), BF)

    @pl.when(no_s)
    def _():
        v_m[:, 18:20] = jnp.zeros((2, 2, 40, 192), BF)
        v_f[:, 33:34] = jnp.zeros((2, 1, 80, 192), BF)

    spans = ((0, 64, no_w), (64, 128, no_e), (128, 144, no_n | no_w), (144, 160, no_n | no_e),
             (160, 176, no_s | no_w), (176, 192, no_s | no_e))
    for lo, hi, gone in spans:
        g32[:, lo:hi, :] = jnp.where(gone, 0.0, v_g[:, lo:hi, :].astype(F32))
    for t in range(2):
        for l, m, base, n, s in ((lf, lm, 0, 128, 160), (rf, rm, 64, 144, 176)):
            l[t, 0:1, :] = g32[t, n : n + 1, :]
            l[t, 1:33, :] = g32[t, base : base + 32, :]
            l[t, 33:34, :] = g32[t, s : s + 1, :]
            for c in range(2):
                m[t, c, 0:2, :] = g32[t, n + 1 + 2 * c : n + 3 + 2 * c, :]
                m[t, c, 2:18, :] = g32[t, base + 32 + 16 * c : base + 48 + 16 * c, :]
                m[t, c, 18:20, :] = g32[t, s + 1 + 2 * c : s + 3 + 2 * c, :]

    for r in range(20):
        buf = rb_m.at[r % 2]
        for t in range(2):
            buf[t, 8:48, :] = v_m[t, r].astype(F32)
            for c in range(2):
                buf[t, 6 + c : 7 + c, :] = lm[t, c, r : r + 1, :]
                buf[t, 48 + c : 49 + c, :] = rm[t, c, r : r + 1, :]
        put_cached(xmc, r * 48, 48, buf, 6)

    def mid_part(i):
        at = i * 288
        k = jnp.concatenate(
            [v[t, r, b] for r in range(3) for v in (v_mf, v_mh) for t in range(2) for b in range(3)], 0)
        acc_m[pl.ds(at, 288), :] = jnp.dot(taps(xmc, at, 288, 48), k, preferred_element_type=F32) + mbias

    for i in range(3):
        mid_part(i)
    fold_weights(v_uk, w4u)
    fold_weights(v_nk, w4n)
    pack_fine(v_fk, wfc, wf2)

    def fine_cached(r):
        buf = rb_f.at[r % 2]
        for t in range(2):
            buf[t, 8:88, :] = v_f[t, r].astype(F32)
            buf[t, 7:8, :] = lf[t, r : r + 1, :]
            buf[t, 88:89, :] = rf[t, r : r + 1, :]
        put_cached(xfc, r * 80, 80, buf, 7)

    for i in range(4):
        for r in range(8 * i + 2 if i else 0, 8 * i + 10):
            fine_cached(r)
        acc_f[i * 640 : i * 640 + 640, :] = nt_dot(taps(xfc, i * 640, 640, 80), wfc[...]) + fbias

    arrived(n_fine, len(copies))
    for t in range(3):
        d_ck[t].wait()
    lane = lax.broadcasted_iota(jnp.int32, (1, 512), 1)
    keep = jnp.logical_and(jnp.logical_or(lane >= 128, a > 0), jnp.logical_or(lane < 384, a < NA - 1))
    for t in range(3):
        for p in range(4):
            part = jnp.where(keep[:, p * 128 : p * 128 + 128],
                             v_coarse[t, :, p * 128 : p * 128 + 128].astype(F32), 0.0)
            flat = part.T
            if t == 2:
                img_l[p * 4 : p * 4 + 4] = flat.reshape(4, 32, 384)
                flat = act(flat, cgain, 384)
            img_c[p * 4 : p * 4 + 4, 0:32, :] = flat.reshape(4, 32, 384)
        for b in range(3):
            v = img_c[1:15, b : b + 24, :].reshape(336, 384)
            for ra in range(3):
                at = (t * 3 + ra) * 288
                xfc[at : at + 288, b * 384 : b * 384 + 384] = v[ra * 24 : ra * 24 + 288].astype(BF)
    total = img_l[2:14, 1:25, :].reshape(288, 384) + cbias
    for t in range(3):
        x = jnp.concatenate([xfc[(t * 3 + ra) * 288 : (t * 3 + ra + 1) * 288, :] for ra in range(3)], 1)
        k = jnp.concatenate([v_ck[t, ra, b] for ra in range(3) for b in range(3)], 1)
        total = total + nt_dot(x, k)
    rid = lax.broadcasted_iota(jnp.int32, (12, 24, 1), 0) + (a * 8 - 2)
    cid = lax.broadcasted_iota(jnp.int32, (12, 24, 1), 1) + (w * 20 - 2)
    inside = (rid >= 0) & (rid < 128) & (cid >= 0) & (cid < 160)
    img1[:, 0:24, :] = jnp.where(inside, total.reshape(12, 24, 384), 0.0)
    for b in range(2):
        xmc[0:384, b * 384 : b * 384 + 384] = img1[:, b : b + 32, :].reshape(384, 384).astype(BF)

    x = jnp.concatenate([xmc[0:352, 0:768], xmc[32:384, 0:768]], 1)
    u = nt_dot(x, w4u[...])
    for i in range(11):
        put_phases(u[i * 32 : i * 32 + 32, :], ubias, img_m, 2 * i, 5)

    mcol = lax.broadcasted_iota(jnp.int32, (72, 1), 0) + (w * 40 - 8)
    mcol = jnp.where((mcol >= 0) & (mcol < 320), 1.0, 0.0)

    def mid_row(r):
        row = a * 16 - 2 + r
        ok = jnp.where((row >= 0) & (row < 256), 1.0, 0.0)
        buf = rb_1.at[r % 4]
        buf[0:72, :] = act(image_row(img_m, r + 1, slice(0, 72)), mgain, 192) * (mcol * ok)
        put_current(xm2, r * 48, 48, buf, 6)

    def bypass_row(r):
        xmc[r * 48 : r * 48 + 48, 768:960] = image_row(img_m, r + 2, slice(7, 55)).astype(BF)

    def mid_block(i):
        at = i * 288
        zero = jnp.zeros((64, 384), BF)
        k = jnp.concatenate(
            [p for r in range(3) for p in
             [v_mf[2, r, b] for b in range(3)] + [v_mh[2, r, b] for b in range(3)] + [zero]], 0)
        total = (acc_m[pl.ds(at, 288), :]
                 + jnp.dot(xmc[pl.ds(at, 288), 768:960], v_bk[...], preferred_element_type=F32)
                 + jnp.dot(taps(xm2, at, 288, 48), k, preferred_element_type=F32))
        rid = lax.broadcasted_iota(jnp.int32, (6, 48, 1), 0) + (a * 16 - 1 + i * 6)
        cid = lax.broadcasted_iota(jnp.int32, (6, 48, 1), 1) + (w * 40 - 1)
        inside = (rid >= 0) & (rid < 256) & (cid >= 0) & (cid < 320)
        img2[i * 6 : i * 6 + 6, 0:48, :] = jnp.where(inside, total.reshape(6, 48, 384), 0.0)
        for r in range(i * 6, i * 6 + 6):
            for b in range(2):
                xmc[r * 48 : r * 48 + 48, b * 384 : b * 384 + 384] = img2[r, b : b + 48, :].astype(BF)

    xmc[864:912, 0:768] = jnp.zeros((48, 768), BF)
    for i in range(3):
        for r in range(6 * i + 2 if i else 0, 6 * i + 8):
            mid_row(r)
        for r in range(6 * i, 6 * i + 6):
            bypass_row(r)
        mid_block(i)

    def fine_block(i):
        at = i * 288
        x = jnp.concatenate([xmc[at : at + 288, 0:768], xmc[at + 48 : at + 336, 0:768]], 1)
        u = nt_dot(x, w4n[...])
        for j in range(6):
            put_phases(u[j * 48 : j * 48 + 48, :], nbias, img_f, i * 12 + 2 * j, 7)

    fcol = lax.broadcasted_iota(jnp.int32, (96, 1), 0) + (w * 80 - 8)
    fcol = jnp.where((fcol >= 0) & (fcol < 640), 1.0, 0.0)

    def fine_rows(first, last):
        for r in range(first, last):
            row = a * 32 - 1 + r
            ok = jnp.where((row >= 0) & (row < 512), 1.0, 0.0)
            buf = rb_1.at[r % 4]
            buf[0:96, :] = act(image_row(img_f, r, slice(0, 96)), fgain, 192) * (fcol * ok)
            put_current(xf2, r * 80, 80, buf, 7)

    def out_block(i):
        at = i * 640
        total = (image_row(img_f, slice(1 + i * 8, 9 + i * 8), slice(8, 88)).reshape(640, 192)
                 + acc_f[at : at + 640, :] + nt_dot(taps(xf2, at, 640, 80), wf2[...]))
        v_f[0, i * 8 : i * 8 + 8] = total.reshape(8, 80, 192).astype(BF)

    fine_block(0)
    fine_block(1)
    fine_rows(0, 12)
    fine_block(2)
    out_block(0)
    fine_rows(12, 24)
    out_block(1)
    fine_rows(24, 34)
    out_block(2)
    out_block(3)
    done = pltpu.make_async_copy(v_f.at[0, pl.ds(0, 32)], out, osem)
    done.start()
    for c, cs, _ in copies:
        if cs is None:
            c.wait_send()
        else:
            pl.when(cs)(c.wait_send)
    done.wait()


def call(*args):
    anywhere = pl.BlockSpec(memory_space=pl.ANY)
    vmem = pl.BlockSpec(memory_space=pltpu.VMEM)
    V = pltpu.VMEM
    n = 10 + 7 + 16
    return pl.pallas_call(
        kernel,
        out_shape=jax.ShapeDtypeStruct((32, 80, 192), BF),
        in_specs=[vmem] * 11 + [anywhere] * 8,
        out_specs=anywhere,
        scratch_shapes=[
            V((3, 384, 512), BF), V((2, 34, 80, 192), BF), V((2, 20, 40, 192), BF), V((2, 192, 192), BF),
            V((3, 3, 3, 384, 384), BF), V((3, 3, 192, 384), BF),
            V((3, 3, 3, 128, 384), BF), V((3, 3, 3, 64, 384), BF),
            V((192, 384), BF), V((3, 3, 192, 384), BF), V((3, 3, 3, 192, 192), BF),
            V((48, 8, 128), F32), V((48, 8, 128), F32), V((2, 192, 192), F32), V((2, 192, 192), BF), V((8, 3, 48, 256), BF),
            V((192, 3456), BF), V((192, 1920), BF), V((768, 1536), BF), V((768, 1536), BF),
            V((2720, 1152), BF), V((2720, 640), BF), V((960, 1152), BF), V((960, 640), BF),
            V((16, 40, 384), F32), V((16, 32, 384), F32), V((12, 40, 384), F32), V((2, 22, 72, 128), F32),
            V((18, 56, 384), F32), V((2, 36, 104, 128), F32), V((2, 2, 96, 192), F32), V((2, 2, 72, 192), F32),
            V((4, 96, 192), F32), V((2, 192, 192), F32),
            V((2, 40, 192), F32), V((2, 40, 192), F32), V((2, 2, 24, 192), F32), V((2, 2, 24, 192), F32),
            V((2560, 192), F32), V((864, 384), F32),
            pltpu.SemaphoreType.DMA((16,)), pltpu.SemaphoreType.DMA,
            pltpu.SemaphoreType.DMA((n,)), pltpu.SemaphoreType.DMA((n,)),
        ],
        compiler_params=pltpu.CompilerParams(
            collective_id=0, has_side_effects=True, vmem_limit_bytes=63 * 2**20),
    )(*args)


def per_device(
    latent_map, coarse_cache, coarse_gain, coarse_kernel, coarse_bias, upper_kernel, upper_bias,
    middle_cache, middle_gain, middle_kernel, middle_bias, bypass_weight, bypass_bias,
    finer_kernel, finer_bias, fine_cache, fine_gain, fine_kernel, fine_bias,
):
    ft = jnp.transpose(fine_cache, (0, 2, 3, 1))
    mt = jnp.transpose(middle_cache, (0, 2, 3, 1))
    y = call(
        latent_map, coarse_cache, coarse_gain, coarse_bias, upper_bias, middle_gain, middle_bias, bypass_bias,
        finer_bias, fine_gain, fine_bias, ft, mt, coarse_kernel, upper_kernel,
        jnp.transpose(middle_kernel, (0, 1, 2, 4, 3)), bypass_weight.T, finer_kernel, fine_kernel)
    return jnp.transpose(y, (2, 0, 1))


def solution(mesh):
    high = (P("wa", "ha", None), P(None, "wa", "ha", None))
    low = P(None, None, "ha", "wa")
    placed = high + (P(),) * 5 + (low,) + (P(),) * 7 + (low,) + (P(),) * 3
    return jax.shard_map(
        per_device, mesh=mesh, in_specs=placed, out_specs=P(None, "ha", "wa"), check_vma=False
    )
```

```python
import jax
import jax.numpy as jnp
from jax import lax
from jax.experimental import pallas as pl
from jax.experimental.pallas import tpu as pltpu
from jax.sharding import PartitionSpec as P

BF = jnp.bfloat16
F32 = jnp.float32
MESH = pl.DeviceIdType.MESH
NA, NW = 16, 8
EPS = 1e-06
NT = (((1,), (1,)), ((), ()))


def act(v, g, channels):
    ms = jnp.sum(v * v, axis=1, keepdims=True) * (1.0 / channels)
    u = v * lax.rsqrt(ms + EPS) * g
    return 0.5 * u * (1.0 + jnp.tanh(0.5 * u))


def nt_dot(x, w):
    return lax.dot_general(x, w, NT, preferred_element_type=F32)


def fold_weights(raw, out):
    def chunk(src, first, step):
        k = [[raw[a, b, pl.ds(src, 16), :].astype(F32) for b in range(3)] for a in range(3)]
        rowed = [[[k[0][b] + k[1][b] for b in range(3)], k[2]],
                 [k[0], [k[1][b] + k[2][b] for b in range(3)]]]
        for sr in range(2):
            for sc in range(2):
                at = first + (sr * 2 + sc) * step
                for ta in range(2):
                    r = rowed[sr][ta]
                    cols = [r[0] + r[1], r[2]] if sc == 0 else [r[0], r[1] + r[2]]
                    for tb in range(2):
                        lane = (ta * 2 + tb) * 384
                        out[pl.ds(at, 16), lane : lane + 384] = cols[tb].astype(BF)

    for c in range(8):
        chunk(c * 16, c * 16, 128)
    for c in range(4):
        chunk(128 + c * 16, 512 + c * 16, 64)


def put_phases(block, bias, img, row, first):
    n = block.shape[0]
    lo, hi = bias[:, 0:128], bias[:, 128:192]
    for s in range(4):
        at = pl.ds(first + s % 2, n, stride=2)
        img[0, row + s // 2, at, :] = block[:, s * 128 : s * 128 + 128] + lo
        high = block[:, 512 + s * 64 : 576 + s * 64] + hi
        img[1, row + s // 2, at, :] = jnp.concatenate([high, jnp.zeros((n, 64), F32)], 1)


def image_row(img, row, cols):
    return jnp.concatenate([img[0, row, cols, :], img[1, row, cols, 0:64]], -1)


def pack_fine(raw, cached, current):
    n = cached.shape[0]
    for a in range(3):
        c = a * 1152
        for t in range(2):
            for b in range(3):
                i = t * 3 + b
                cached[:, c + i * 128 : c + i * 128 + 128] = raw[t, a, b, :, 0:128]
        for i in range(3):
            p, q = 2 * i, 2 * i + 1
            cached[:, c + 768 + i * 128 : c + 896 + i * 128] = jnp.concatenate(
                [raw[p // 3, a, p % 3, :, 128:192], raw[q // 3, a, q % 3, :, 128:192]], 1)
        c = a * 512
        for b in range(3):
            current[:, c + b * 128 : c + b * 128 + 128] = raw[2, a, b, :, 0:128]
        current[:, c + 384 : c + 512] = jnp.concatenate([raw[2, a, 0, :, 128:192], raw[2, a, 1, :, 128:192]], 1)
    current[:, 1536:1664] = jnp.concatenate([raw[2, 0, 2, :, 128:192], raw[2, 1, 2, :, 128:192]], 1)
    current[:, 1664:1792] = jnp.concatenate([raw[2, 2, 2, :, 128:192], jnp.zeros((n, 64), BF)], 1)


def put_cached(x, at, n, buf, first):
    v = [buf[i // 3, first + i % 3 : first + i % 3 + n, :].astype(BF) for i in range(6)]
    rows = pl.ds(at, n)
    for i in range(6):
        x[rows, i * 128 : i * 128 + 128] = v[i][:, 0:128]
    for i in range(3):
        x[rows, 768 + i * 128 : 896 + i * 128] = jnp.concatenate(
            [v[2 * i][:, 128:192], v[2 * i + 1][:, 128:192]], 1)


def put_current(x, xh, r, rows, n, buf, first):
    v = [buf[first + b : first + b + n, :].astype(BF) for b in range(3)]
    at = slice(r * n, r * n + n)
    for b in range(3):
        x[at, b * 128 : b * 128 + 128] = v[b][:, 0:128]
    x[at, 384:512] = jnp.concatenate([v[0][:, 128:192], v[1][:, 128:192]], 1)
    for tap in range(3):
        if 0 <= r - tap < rows:
            xh[(r - tap) * n : (r - tap) * n + n, tap * 64 : tap * 64 + 64] = v[2][:, 128:192]


def taps(x, at, n, pitch):
    return jnp.concatenate([x[pl.ds(at + r * pitch, n), :] for r in range(3)], 1)


def kernel(
    lat, cc, g_c, b_c, b_u, g_m, b_m, b_b, b_n, g_f, b_f, ft, mt, ck, uk, mk, bk, nk, fk,
    out,
    v_coarse, v_f, v_m, v_g, v_ck, v_uk, v_mf, v_mh, v_bk, v_nk, v_fk,
    s0, s1, e32, edge, pack, wfc, wf2, w4u, w4n, xfc, xf2, xfh, xmc, xm2, xmh,
    img_c, img_l, img1, img_m, img2, img_f, rb_f, rb_m, rb_1, g32,
    lf, rf, lm, rm, acc_f, acc_m, sem, osem, send, recv,
):
    a = lax.axis_index("ha")
    w = lax.axis_index("wa")
    north, south = a > 0, a < NA - 1
    west, east = w > 0, w < NW - 1
    barrier = pltpu.get_barrier_semaphore()

    def greet(da, k):
        pl.semaphore_signal(
            barrier, inc=1, device_id=(a + da, lax.rem(w + k, NW)), device_id_type=MESH
        )

    count = [0]

    def load(src, dst):
        c = pltpu.make_async_copy(src, dst, sem.at[count[0]])
        count[0] += 1
        c.start()
        return c

    d_m = load(mt, v_m.at[:, pl.ds(2, 16)])
    d_f = load(ft, v_f.at[:, pl.ds(1, 32)])

    for k in range(1, NW):
        greet(0, k)

    @pl.when(north)
    def _():
        for k in range(NW):
            greet(-1, k)

    @pl.when(south)
    def _():
        for k in range(NW):
            greet(1, k)

    quarter = lax.broadcasted_iota(jnp.int32, (1, 128), 1) // 32
    for t in range(3):
        x = (lat[...] if t == 2 else cc[t]).astype(F32)
        s0[...] = x[:, :, 0:128]
        s1[...] = jnp.concatenate([x[:, :, 128:160], jnp.zeros((48, 8, 96), F32)], 2)
        for half in range(2):
            rows4 = [jnp.concatenate([s0[:, half * 4 + h, :], s1[:, half * 4 + h, :]], 1) for h in range(4)]
            for to in range(NW):
                got = None
                for h in range(4):
                    shift = (half * 128 + h * 32 - (20 * to - 3)) % 256
                    moved = pltpu.roll(rows4[h], shift, 1)[:, half * 128 : half * 128 + 128]
                    got = moved if got is None else jnp.where(quarter == h, moved, got)
                pack[to, t, :, half * 128 : half * 128 + 128] = got.astype(BF)

    def column(ref, t, first, n, tile, col):
        x = ref[t, first : first + n, tile : tile + 8, :].astype(F32)
        s0[0:n] = x[:, :, 0:128]
        s1[0:n] = jnp.concatenate([x[:, :, 128:192], jnp.zeros((n, 8, 64), F32)], 2)
        return [jnp.concatenate([s0[0:n, c, :], s1[0:n, c, 0:64]], 1) for c in col]

    d_m.wait()
    d_f.wait()
    e32[:, 128:192, :] = jnp.zeros((2, 64, 192), F32)
    for t in range(2):
        for side in range(2):
            (f,) = column(v_f, t, 1, 32, 72 - 72 * side, (7 - 7 * side,))
            m = column(v_m, t, 2, 16, 32 - 32 * side, (6 - 6 * side, 7 - 6 * side))
            e32[t, 64 * side : 64 * side + 32, :] = f
            e32[t, 64 * side + 32 : 64 * side + 48, :] = m[0]
            e32[t, 64 * side + 48 : 64 * side + 64, :] = m[1]
            for north_end in range(2):
                at = 128 + 32 * north_end + 16 * side
                h, r = 31 - 31 * north_end, 14 - 14 * north_end
                e32[t, at : at + 1, :] = f[h : h + 1]
                e32[t, at + 1 : at + 3, :] = m[0][r : r + 2]
                e32[t, at + 3 : at + 5, :] = m[1][r : r + 2]
    edge[...] = e32[...].astype(BF)

    pl.semaphore_wait(barrier, NW - 1 + NW * (jnp.where(north, 1, 0) + jnp.where(south, 1, 0)))

    mine = pl.ds(pl.multiple_of(w * 48, 16), 48)
    copies = []

    def remote(src, dst, da, to_w, cond_send, cond_recv):
        s = len(copies)
        c = pltpu.make_async_remote_copy(
            src_ref=src, dst_ref=dst, send_sem=send.at[s], recv_sem=recv.at[s],
            device_id=(a + da, to_w), device_id_type=MESH)
        copies.append((c, cond_send, cond_recv))

    remote(edge.at[:, pl.ds(0, 64)], v_g.at[:, pl.ds(0, 64)], 0, w + 1, east, west)
    remote(edge.at[:, pl.ds(64, 64)], v_g.at[:, pl.ds(64, 64)], 0, w - 1, west, east)
    for i, (da, dw) in enumerate(((1, 1), (1, -1), (-1, 1), (-1, -1))):
        go_a, from_a = (south, north) if da == 1 else (north, south)
        go_w, from_w = (east, west) if dw == 1 else (west, east)
        strip = pl.ds(128 + 16 * i, 16)
        remote(edge.at[:, strip], v_g.at[:, strip], da, w + dw,
               jnp.logical_and(go_a, go_w), jnp.logical_and(from_a, from_w))
    n_edge = len(copies)
    remote(mt.at[:, pl.ds(14, 2)], v_m.at[:, pl.ds(0, 2)], 1, w, south, north)
    remote(mt.at[:, pl.ds(0, 2)], v_m.at[:, pl.ds(18, 2)], -1, w, north, south)
    n_mid = len(copies)
    remote(ft.at[:, 31], v_f.at[:, 0], 1, w, south, north)
    remote(ft.at[:, 0], v_f.at[:, 33], -1, w, north, south)
    n_fine = len(copies)

    def begin(first, last):
        for c, cs, _ in copies[first:last]:
            if cs is None:
                c.start()
            else:
                pl.when(cs)(c.start)

    begin(0, n_fine)

    odd = lax.rem(a, 2) == 1
    even = jnp.logical_not(odd)
    for k in range(1, NW):
        to = lax.rem(w + k, NW)
        remote(pack.at[to], v_coarse.at[:, mine, pl.ds(128, 256)], 0, to, None, None)
    n_main = len(copies)
    for k in range(NW):
        to = lax.rem(w + k, NW)
        remote(pack.at[to, :, :, pl.ds(128, 128)], v_coarse.at[:, mine, pl.ds(0, 128)], 1, to,
               jnp.logical_and(odd, south), jnp.logical_and(even, north))
        remote(pack.at[to, :, :, pl.ds(0, 128)], v_coarse.at[:, mine, pl.ds(384, 128)], -1, to,
               jnp.logical_and(even, north), jnp.logical_and(odd, south))
    n_far = len(copies)
    remote(v_coarse.at[:, :, pl.ds(256, 128)], v_coarse.at[:, :, pl.ds(0, 128)], 1, w, even, odd)
    remote(v_coarse.at[:, :, pl.ds(128, 128)], v_coarse.at[:, :, pl.ds(384, 128)], -1, w, odd, even)
    begin(n_fine, n_far)
    d_uk = load(uk, v_uk)
    d_nk = load(nk, v_nk)
    d_fk = load(fk, v_fk)
    d_mf = load(mk.at[:, :, :, pl.ds(0, 128), :], v_mf)
    d_mh = load(mk.at[:, :, :, pl.ds(128, 64), :], v_mh)
    d_bk = load(bk, v_bk)
    d_ck = [load(ck.at[t], v_ck.at[t]) for t in range(3)]

    def arrived(first, last):
        for c, _, cr in copies[first:last]:
            if cr is None:
                c.wait_recv()
            else:
                pl.when(cr)(c.wait_recv)

    v_coarse[:, mine, 128:384] = pack[w]
    cgain, cbias, ubias, mgain, mbias, bbias, nbias, fgain, fbias = [
        v[...].reshape(1, -1) for v in (g_c, b_c, b_u, g_m, b_m, b_b, b_n, g_f, b_f)]
    mbias = mbias + bbias

    xfh[:, 128:256] = jnp.zeros((2560, 128), BF)
    xmh[:, 128:256] = jnp.zeros((864, 128), BF)
    img1[...] = jnp.zeros_like(img1)
    rb_m[...] = jnp.zeros_like(rb_m)
    rb_1[...] = jnp.zeros_like(rb_1)
    img_m[...] = jnp.zeros_like(img_m)

    d_uk.wait()
    fold_weights(v_uk, w4u)
    d_nk.wait()
    fold_weights(v_nk, w4n)
    d_fk.wait()
    pack_fine(v_fk, wfc, wf2)

    def fine_cached(r, beside):
        buf = rb_f.at[r % 2]
        for t in range(2):
            buf[t, 8:88, :] = v_f[t, r].astype(F32)
            if beside:
                buf[t, 7:8, :] = lf[t, r : r + 1, :]
                buf[t, 88:89, :] = rf[t, r : r + 1, :]
        put_cached(xfc, r * 80, 80, buf, 7)

    rb_f[...] = jnp.zeros_like(rb_f)
    xfc[0:80, :] = jnp.zeros((80, 1152), BF)
    xfc[2640:2720, :] = jnp.zeros((80, 1152), BF)
    for i in range(4):
        for r in range(8 * i + 2 if i else 1, min(8 * i + 10, 33)):
            fine_cached(r, False)
        acc_f[i * 640 : i * 640 + 640, :] = nt_dot(taps(xfc, i * 640, 640, 80), wfc[...]) + fbias
    d_mf.wait()
    d_mh.wait()
    d_bk.wait()

    arrived(0, n_fine)
    no_n, no_s, no_w, no_e = a == 0, a == NA - 1, w == 0, w == NW - 1

    @pl.when(no_n)
    def _():
        v_m[:, 0:2] = jnp.zeros((2, 2, 40, 192), BF)
        v_f[:, 0:1] = jnp.zeros((2, 1, 80, 192), BF)

    @pl.when(no_s)
    def _():
        v_m[:, 18:20] = jnp.zeros((2, 2, 40, 192), BF)
        v_f[:, 33:34] = jnp.zeros((2, 1, 80, 192), BF)

    spans = ((0, 64, no_w), (64, 128, no_e), (128, 144, no_n | no_w), (144, 160, no_n | no_e),
             (160, 176, no_s | no_w), (176, 192, no_s | no_e))
    for lo, hi, gone in spans:
        g32[:, lo:hi, :] = jnp.where(gone, 0.0, v_g[:, lo:hi, :].astype(F32))
    for t in range(2):
        for l, m, base, n, s in ((lf, lm, 0, 128, 160), (rf, rm, 64, 144, 176)):
            l[t, 0:1, :] = g32[t, n : n + 1, :]
            l[t, 1:33, :] = g32[t, base : base + 32, :]
            l[t, 33:34, :] = g32[t, s : s + 1, :]
            for c in range(2):
                m[t, c, 0:2, :] = g32[t, n + 1 + 2 * c : n + 3 + 2 * c, :]
                m[t, c, 2:18, :] = g32[t, base + 32 + 16 * c : base + 48 + 16 * c, :]
                m[t, c, 18:20, :] = g32[t, s + 1 + 2 * c : s + 3 + 2 * c, :]

    for r in (0, 33):
        fine_cached(r, True)
    acc_f[0:80, :] += nt_dot(xfc[0:80, :], wfc[:, 0:1152])
    acc_f[2480:2560, :] += nt_dot(xfc[2640:2720, :], wfc[:, 2304:3456])
    own_row = lax.broadcasted_iota(jnp.int32, (40, 1), 0)
    own_row = (own_row >= 1) & (own_row <= 32)
    for l, col, b in ((lf, 0, 0), (rf, 79, 2)):
        beside = jnp.zeros((32, 192), F32)
        for t in range(2):
            v = jnp.where(own_row, l[t], 0.0)
            for ra in range(3):
                beside = beside + nt_dot(v[ra : ra + 32].astype(BF), v_fk[t, ra, b])
        for h in range(32):
            acc_f[h * 80 + col : h * 80 + col + 1, :] += beside[h : h + 1]

    for r in range(20):
        buf = rb_m.at[r % 2]
        for t in range(2):
            buf[t, 8:48, :] = v_m[t, r].astype(F32)
            for c in range(2):
                buf[t, 6 + c : 7 + c, :] = lm[t, c, r : r + 1, :]
                buf[t, 48 + c : 49 + c, :] = rm[t, c, r : r + 1, :]
        put_cached(xmc, r * 48, 48, buf, 6)

    def mid_part(at, n):
        k = jnp.concatenate(
            [v[t, r, b] for r in range(3) for v in (v_mf, v_mh) for t in range(2) for b in range(3)], 0)
        acc_m[at : at + n, :] = jnp.dot(taps(xmc, at, n, 48), k, preferred_element_type=F32) + mbias

    mid_part(0, 864)
    arrived(n_fine, n_main)
    begin(n_far, len(copies))

    arrived(n_main, len(copies))
    for t in range(3):
        d_ck[t].wait()
    lane = lax.broadcasted_iota(jnp.int32, (1, 512), 1)
    keep = jnp.logical_and(jnp.logical_or(lane >= 128, a > 0), jnp.logical_or(lane < 384, a < NA - 1))
    for t in range(3):
        for p in range(4):
            part = jnp.where(keep[:, p * 128 : p * 128 + 128],
                             v_coarse[t, :, p * 128 : p * 128 + 128].astype(F32), 0.0)
            flat = part.T
            if t == 2:
                img_l[p * 4 : p * 4 + 4] = flat.reshape(4, 32, 384)
                flat = act(flat, cgain, 384)
            img_c[p * 4 : p * 4 + 4, 0:32, :] = flat.reshape(4, 32, 384)
        for b in range(3):
            v = img_c[1:15, b : b + 24, :].reshape(336, 384)
            for ra in range(3):
                at = (t * 3 + ra) * 288
                xfc[at : at + 288, b * 384 : b * 384 + 384] = v[ra * 24 : ra * 24 + 288].astype(BF)
    total = img_l[2:14, 1:25, :].reshape(288, 384) + cbias
    for t in range(3):
        x = jnp.concatenate([xfc[(t * 3 + ra) * 288 : (t * 3 + ra + 1) * 288, :] for ra in range(3)], 1)
        k = jnp.concatenate([v_ck[t, ra, b] for ra in range(3) for b in range(3)], 1)
        total = total + nt_dot(x, k)
    rid = lax.broadcasted_iota(jnp.int32, (12, 24, 1), 0) + (a * 8 - 2)
    cid = lax.broadcasted_iota(jnp.int32, (12, 24, 1), 1) + (w * 20 - 2)
    inside = (rid >= 0) & (rid < 128) & (cid >= 0) & (cid < 160)
    img1[:, 0:24, :] = jnp.where(inside, total.reshape(12, 24, 384), 0.0)
    for b in range(2):
        xmc[0:384, b * 384 : b * 384 + 384] = img1[:, b : b + 32, :].reshape(384, 384).astype(BF)

    x = jnp.concatenate([xmc[0:352, 0:768], xmc[32:384, 0:768]], 1)
    u = nt_dot(x, w4u[...])
    for i in range(11):
        put_phases(u[i * 32 : i * 32 + 32, :], ubias, img_m, 2 * i, 5)

    mcol = lax.broadcasted_iota(jnp.int32, (72, 1), 0) + (w * 40 - 8)
    mcol = jnp.where((mcol >= 0) & (mcol < 320), 1.0, 0.0)

    def mid_row(r):
        row = a * 16 - 2 + r
        ok = jnp.where((row >= 0) & (row < 256), 1.0, 0.0)
        buf = rb_1.at[r % 4]
        buf[0:72, :] = act(image_row(img_m, r + 1, slice(0, 72)), mgain, 192) * (mcol * ok)
        put_current(xm2, xmh, r, 18, 48, buf, 6)

    def bypass_row(r):
        xmc[r * 48 : r * 48 + 48, 768:960] = image_row(img_m, r + 2, slice(7, 55)).astype(BF)

    def mid_block(i):
        at = i * 432
        k = jnp.concatenate(
            [p for r in range(3) for p in
             [v_mf[2, r, b] for b in range(3)] + [v_mh[2, r, b] for b in range(2)]]
            + [v_mh[2, r, 2] for r in range(3)] + [jnp.zeros((64, 384), BF)], 0)
        x = jnp.concatenate([taps(xm2, at, 432, 48), xmh[at : at + 432, :]], 1)
        total = (acc_m[at : at + 432, :]
                 + jnp.dot(xmc[at : at + 432, 768:960], v_bk[...], preferred_element_type=F32)
                 + jnp.dot(x, k, preferred_element_type=F32))
        rid = lax.broadcasted_iota(jnp.int32, (9, 48, 1), 0) + (a * 16 - 1 + i * 9)
        cid = lax.broadcasted_iota(jnp.int32, (9, 48, 1), 1) + (w * 40 - 1)
        inside = (rid >= 0) & (rid < 256) & (cid >= 0) & (cid < 320)
        img2[i * 9 : i * 9 + 9, 0:48, :] = jnp.where(inside, total.reshape(9, 48, 384), 0.0)
        for r in range(i * 9, i * 9 + 9):
            for b in range(2):
                xmc[r * 48 : r * 48 + 48, b * 384 : b * 384 + 384] = img2[r, b : b + 48, :].astype(BF)

    def fine_block(first, n):
        at, m = first * 48, n * 48
        x = jnp.concatenate([xmc[at : at + m, 0:768], xmc[at + 48 : at + 48 + m, 0:768]], 1)
        u = nt_dot(x, w4n[...])
        for j in range(n):
            put_phases(u[j * 48 : j * 48 + 48, :], nbias, img_f, 2 * (first + j), 7)

    dones = []
    fcol = lax.broadcasted_iota(jnp.int32, (96, 1), 0) + (w * 80 - 8)
    fcol = jnp.where((fcol >= 0) & (fcol < 640), 1.0, 0.0)

    def fine_rows(first, last):
        for r in range(first, last):
            row = a * 32 - 1 + r
            ok = jnp.where((row >= 0) & (row < 512), 1.0, 0.0)
            buf = rb_1.at[r % 4]
            buf[0:96, :] = act(image_row(img_f, r, slice(0, 96)), fgain, 192) * (fcol * ok)
            put_current(xf2, xfh, r, 32, 80, buf, 7)

    def out_block(i):
        at = i * 640
        total = (image_row(img_f, slice(1 + i * 8, 9 + i * 8), slice(8, 88)).reshape(640, 192)
                 + acc_f[at : at + 640, :] + nt_dot(
                     jnp.concatenate([taps(xf2, at, 640, 80), xfh[at : at + 640, :]], 1), wf2[...]))
        v_f[0, i * 8 : i * 8 + 8] = total.reshape(8, 80, 192).astype(BF)
        rows = pl.ds(i * 8, 8)
        done = pltpu.make_async_copy(v_f.at[0, rows], out.at[rows], osem.at[i])
        done.start()
        dones.append(done)

    for r in range(11):
        mid_row(r)
    for r in range(9):
        bypass_row(r)
    mid_block(0)
    for r in range(11, 20):
        mid_row(r)
    for r in range(9, 18):
        bypass_row(r)
    fine_block(0, 8)
    mid_block(1)
    fine_rows(0, 16)
    fine_block(8, 9)
    out_block(0)
    fine_rows(16, 26)
    out_block(1)
    fine_rows(26, 34)
    out_block(2)
    out_block(3)
    for c, cs, _ in copies:
        if cs is None:
            c.wait_send()
        else:
            pl.when(cs)(c.wait_send)
    for done in dones:
        done.wait()


def call(*args):
    anywhere = pl.BlockSpec(memory_space=pl.ANY)
    vmem = pl.BlockSpec(memory_space=pltpu.VMEM)
    V = pltpu.VMEM
    n = 10 + 7 + 16 + 2
    return pl.pallas_call(
        kernel,
        out_shape=jax.ShapeDtypeStruct((32, 80, 192), BF),
        in_specs=[vmem] * 11 + [anywhere] * 8,
        out_specs=anywhere,
        scratch_shapes=[
            V((3, 384, 512), BF), V((2, 34, 80, 192), BF), V((2, 20, 40, 192), BF), V((2, 192, 192), BF),
            V((3, 3, 3, 384, 384), BF), V((3, 3, 192, 384), BF),
            V((3, 3, 3, 128, 384), BF), V((3, 3, 3, 64, 384), BF),
            V((192, 384), BF), V((3, 3, 192, 384), BF), V((3, 3, 3, 192, 192), BF),
            V((48, 8, 128), F32), V((48, 8, 128), F32), V((2, 192, 192), F32), V((2, 192, 192), BF), V((8, 3, 48, 256), BF),
            V((192, 3456), BF), V((192, 1792), BF), V((768, 1536), BF), V((768, 1536), BF),
            V((2720, 1152), BF), V((2720, 512), BF), V((2560, 256), BF), V((960, 1152), BF), V((960, 512), BF), V((864, 256), BF),
            V((16, 40, 384), F32), V((16, 32, 384), F32), V((12, 40, 384), F32), V((2, 22, 72, 128), F32),
            V((18, 56, 384), F32), V((2, 34, 104, 128), F32), V((2, 2, 96, 192), F32), V((2, 2, 72, 192), F32),
            V((4, 96, 192), F32), V((2, 192, 192), F32),
            V((2, 40, 192), F32), V((2, 40, 192), F32), V((2, 2, 24, 192), F32), V((2, 2, 24, 192), F32),
            V((2560, 192), F32), V((864, 384), F32),
            pltpu.SemaphoreType.DMA((16,)), pltpu.SemaphoreType.DMA((4,)),
            pltpu.SemaphoreType.DMA((n,)), pltpu.SemaphoreType.DMA((n,)),
        ],
        compiler_params=pltpu.CompilerParams(
            collective_id=0, has_side_effects=True, vmem_limit_bytes=63 * 2**20),
    )(*args)


def per_device(
    latent_map, coarse_cache, coarse_gain, coarse_kernel, coarse_bias, upper_kernel, upper_bias,
    middle_cache, middle_gain, middle_kernel, middle_bias, bypass_weight, bypass_bias,
    finer_kernel, finer_bias, fine_cache, fine_gain, fine_kernel, fine_bias,
):
    ft = jnp.transpose(fine_cache, (0, 2, 3, 1))
    mt = jnp.transpose(middle_cache, (0, 2, 3, 1))
    y = call(
        latent_map, coarse_cache, coarse_gain, coarse_bias, upper_bias, middle_gain, middle_bias, bypass_bias,
        finer_bias, fine_gain, fine_bias, ft, mt, coarse_kernel, upper_kernel,
        jnp.transpose(middle_kernel, (0, 1, 2, 4, 3)), bypass_weight.T, finer_kernel, fine_kernel)
    return jnp.transpose(y, (2, 0, 1))


def solution(mesh):
    high = (P("wa", "ha", None), P(None, "wa", "ha", None))
    low = P(None, None, "ha", "wa")
    placed = high + (P(),) * 5 + (low,) + (P(),) * 7 + (low,) + (P(),) * 3
    return jax.shard_map(
        per_device, mesh=mesh, in_specs=placed, out_specs=P(None, "ha", "wa"), check_vma=False
    )
```

```python
import jax
import jax.numpy as jnp
from jax import lax
from jax.experimental import pallas as pl
from jax.experimental.pallas import tpu as pltpu
from jax.sharding import PartitionSpec as P

BF = jnp.bfloat16
F32 = jnp.float32
MESH = pl.DeviceIdType.MESH
NA, NW = 16, 8
EPS = 1e-06
NT = (((1,), (1,)), ((), ()))


def act(v, g, channels):
    ms = jnp.sum(v * v, axis=1, keepdims=True) * (1.0 / channels)
    u = v * lax.rsqrt(ms + EPS) * g
    return 0.5 * u * (1.0 + jnp.tanh(0.5 * u))


def nt_dot(x, w):
    return lax.dot_general(x, w, NT, preferred_element_type=F32)


def fold_weights(raw, out):
    def chunk(src, first, step):
        k = [[raw[a, b, pl.ds(src, 16), :].astype(F32) for b in range(3)] for a in range(3)]
        rowed = [[[k[0][b] + k[1][b] for b in range(3)], k[2]],
                 [k[0], [k[1][b] + k[2][b] for b in range(3)]]]
        for sr in range(2):
            for sc in range(2):
                at = first + (sr * 2 + sc) * step
                for ta in range(2):
                    r = rowed[sr][ta]
                    cols = [r[0] + r[1], r[2]] if sc == 0 else [r[0], r[1] + r[2]]
                    for tb in range(2):
                        lane = (ta * 2 + tb) * 384
                        out[pl.ds(at, 16), lane : lane + 384] = cols[tb].astype(BF)

    for c in range(8):
        chunk(c * 16, c * 16, 128)
    for c in range(4):
        chunk(128 + c * 16, 512 + c * 16, 64)


def put_phases(block, bias, img, row, first):
    n = block.shape[0]
    lo, hi = bias[:, 0:128], bias[:, 128:192]
    for s in range(4):
        at = pl.ds(first + s % 2, n, stride=2)
        img[0, row + s // 2, at, :] = block[:, s * 128 : s * 128 + 128] + lo
        high = block[:, 512 + s * 64 : 576 + s * 64] + hi
        img[1, row + s // 2, at, :] = jnp.concatenate([high, jnp.zeros((n, 64), F32)], 1)


def image_row(img, row, cols):
    return jnp.concatenate([img[0, row, cols, :], img[1, row, cols, 0:64]], -1)


def pack_fine(raw, cached, current):
    n = cached.shape[0]
    for a in range(3):
        c = a * 1152
        for t in range(2):
            for b in range(3):
                i = t * 3 + b
                cached[:, c + i * 128 : c + i * 128 + 128] = raw[t, a, b, :, 0:128]
        for i in range(3):
            p, q = 2 * i, 2 * i + 1
            cached[:, c + 768 + i * 128 : c + 896 + i * 128] = jnp.concatenate(
                [raw[p // 3, a, p % 3, :, 128:192], raw[q // 3, a, q % 3, :, 128:192]], 1)
        c = a * 512
        for b in range(3):
            current[:, c + b * 128 : c + b * 128 + 128] = raw[2, a, b, :, 0:128]
        current[:, c + 384 : c + 512] = jnp.concatenate([raw[2, a, 0, :, 128:192], raw[2, a, 1, :, 128:192]], 1)
    current[:, 1536:1664] = jnp.concatenate([raw[2, 0, 2, :, 128:192], raw[2, 1, 2, :, 128:192]], 1)
    current[:, 1664:1792] = jnp.concatenate([raw[2, 2, 2, :, 128:192], jnp.zeros((n, 64), BF)], 1)


def put_cached(x, at, n, buf, first):
    v = [buf[i // 3, first + i % 3 : first + i % 3 + n, :].astype(BF) for i in range(6)]
    rows = pl.ds(at, n)
    for i in range(6):
        x[rows, i * 128 : i * 128 + 128] = v[i][:, 0:128]
    for i in range(3):
        x[rows, 768 + i * 128 : 896 + i * 128] = jnp.concatenate(
            [v[2 * i][:, 128:192], v[2 * i + 1][:, 128:192]], 1)


def put_current(x, xh, r, rows, n, buf, first):
    v = [buf[first + b : first + b + n, :].astype(BF) for b in range(3)]
    at = slice(r * n, r * n + n)
    for b in range(3):
        x[at, b * 128 : b * 128 + 128] = v[b][:, 0:128]
    x[at, 384:512] = jnp.concatenate([v[0][:, 128:192], v[1][:, 128:192]], 1)
    for tap in range(3):
        if 0 <= r - tap < rows:
            xh[(r - tap) * n : (r - tap) * n + n, tap * 64 : tap * 64 + 64] = v[2][:, 128:192]


def taps(x, at, n, pitch):
    return jnp.concatenate([x[pl.ds(at + r * pitch, n), :] for r in range(3)], 1)


def kernel(
    lat, cc, g_c, b_c, b_u, g_m, b_m, b_b, b_n, g_f, b_f, ft, mt, ck, uk, mk, bk, nk, fk,
    out,
    v_coarse, v_f, v_m, v_g, v_ck, v_uk, v_mf, v_mh, v_bk, v_nk, v_fk,
    s0, s1, e32, edge, pack, wfc, wf2, w4u, w4n, xfc, xf2, xfh, xmc, xm2, xmh,
    img_c, img_l, img1, img_m, img2, img_f, rb_f, rb_m, rb_1, g32,
    lf, rf, lm, rm, acc_f, acc_m, sem, osem, send, recv,
):
    a = lax.axis_index("ha")
    w = lax.axis_index("wa")
    north, south = a > 0, a < NA - 1
    west, east = w > 0, w < NW - 1
    barrier = pltpu.get_barrier_semaphore()

    def greet(da, k):
        pl.semaphore_signal(
            barrier, inc=1, device_id=(a + da, lax.rem(w + k, NW)), device_id_type=MESH
        )

    count = [0]

    def load(src, dst):
        c = pltpu.make_async_copy(src, dst, sem.at[count[0]])
        count[0] += 1
        c.start()
        return c

    d_m = load(mt, v_m.at[:, pl.ds(2, 16)])
    d_f = load(ft, v_f.at[:, pl.ds(1, 32)])

    for k in range(1, NW):
        greet(0, k)

    @pl.when(north)
    def _():
        for k in range(NW):
            greet(-1, k)

    @pl.when(south)
    def _():
        for k in range(NW):
            greet(1, k)

    quarter = lax.broadcasted_iota(jnp.int32, (1, 128), 1) // 32
    for t in range(3):
        x = (lat[...] if t == 2 else cc[t]).astype(F32)
        s0[...] = x[:, :, 0:128]
        s1[...] = jnp.concatenate([x[:, :, 128:160], jnp.zeros((48, 8, 96), F32)], 2)
        for half in range(2):
            rows4 = [jnp.concatenate([s0[:, half * 4 + h, :], s1[:, half * 4 + h, :]], 1) for h in range(4)]
            for to in range(NW):
                got = None
                for h in range(4):
                    shift = (half * 128 + h * 32 - (20 * to - 3)) % 256
                    moved = pltpu.roll(rows4[h], shift, 1)[:, half * 128 : half * 128 + 128]
                    got = moved if got is None else jnp.where(quarter == h, moved, got)
                pack[to, t, :, half * 128 : half * 128 + 128] = got.astype(BF)

    def column(ref, t, first, n, tile, col):
        x = ref[t, first : first + n, tile : tile + 8, :].astype(F32)
        s0[0:n] = x[:, :, 0:128]
        s1[0:n] = jnp.concatenate([x[:, :, 128:192], jnp.zeros((n, 8, 64), F32)], 2)
        return [jnp.concatenate([s0[0:n, c, :], s1[0:n, c, 0:64]], 1) for c in col]

    d_m.wait()
    d_f.wait()
    e32[:, 128:192, :] = jnp.zeros((2, 64, 192), F32)
    for t in range(2):
        for side in range(2):
            (f,) = column(v_f, t, 1, 32, 72 - 72 * side, (7 - 7 * side,))
            m = column(v_m, t, 2, 16, 32 - 32 * side, (6 - 6 * side, 7 - 6 * side))
            e32[t, 64 * side : 64 * side + 32, :] = f
            e32[t, 64 * side + 32 : 64 * side + 48, :] = m[0]
            e32[t, 64 * side + 48 : 64 * side + 64, :] = m[1]
            for north_end in range(2):
                at = 128 + 32 * north_end + 16 * side
                h, r = 31 - 31 * north_end, 14 - 14 * north_end
                e32[t, at : at + 1, :] = f[h : h + 1]
                e32[t, at + 1 : at + 3, :] = m[0][r : r + 2]
                e32[t, at + 3 : at + 5, :] = m[1][r : r + 2]
    edge[...] = e32[...].astype(BF)

    pl.semaphore_wait(barrier, NW - 1 + NW * (jnp.where(north, 1, 0) + jnp.where(south, 1, 0)))

    mine = pl.ds(pl.multiple_of(w * 48, 16), 48)
    copies = []

    def remote(src, dst, da, to_w, cond_send, cond_recv):
        s = len(copies)
        c = pltpu.make_async_remote_copy(
            src_ref=src, dst_ref=dst, send_sem=send.at[s], recv_sem=recv.at[s],
            device_id=(a + da, to_w), device_id_type=MESH)
        copies.append((c, cond_send, cond_recv))

    remote(edge.at[:, pl.ds(0, 64)], v_g.at[:, pl.ds(0, 64)], 0, w + 1, east, west)
    remote(edge.at[:, pl.ds(64, 64)], v_g.at[:, pl.ds(64, 64)], 0, w - 1, west, east)
    for i, (da, dw) in enumerate(((1, 1), (1, -1), (-1, 1), (-1, -1))):
        go_a, from_a = (south, north) if da == 1 else (north, south)
        go_w, from_w = (east, west) if dw == 1 else (west, east)
        strip = pl.ds(128 + 16 * i, 16)
        remote(edge.at[:, strip], v_g.at[:, strip], da, w + dw,
               jnp.logical_and(go_a, go_w), jnp.logical_and(from_a, from_w))
    n_edge = len(copies)
    remote(mt.at[:, pl.ds(14, 2)], v_m.at[:, pl.ds(0, 2)], 1, w, south, north)
    remote(mt.at[:, pl.ds(0, 2)], v_m.at[:, pl.ds(18, 2)], -1, w, north, south)
    n_mid = len(copies)
    remote(ft.at[:, 31], v_f.at[:, 0], 1, w, south, north)
    remote(ft.at[:, 0], v_f.at[:, 33], -1, w, north, south)
    n_fine = len(copies)

    def begin(first, last):
        for c, cs, _ in copies[first:last]:
            if cs is None:
                c.start()
            else:
                pl.when(cs)(c.start)

    odd = lax.rem(a, 2) == 1
    even = jnp.logical_not(odd)
    for k in range(1, NW):
        to = lax.rem(w + k, NW)
        remote(pack.at[to], v_coarse.at[:, mine, pl.ds(128, 256)], 0, to, None, None)
    n_main = len(copies)
    for k in range(NW):
        to = lax.rem(w + k, NW)
        remote(pack.at[to, :, :, pl.ds(128, 128)], v_coarse.at[:, mine, pl.ds(0, 128)], 1, to,
               jnp.logical_and(odd, south), jnp.logical_and(even, north))
        remote(pack.at[to, :, :, pl.ds(0, 128)], v_coarse.at[:, mine, pl.ds(384, 128)], -1, to,
               jnp.logical_and(even, north), jnp.logical_and(odd, south))
    n_far = len(copies)
    remote(v_coarse.at[:, :, pl.ds(256, 128)], v_coarse.at[:, :, pl.ds(0, 128)], 1, w, even, odd)
    remote(v_coarse.at[:, :, pl.ds(128, 128)], v_coarse.at[:, :, pl.ds(384, 128)], -1, w, odd, even)
    begin(n_fine, n_far)
    begin(0, n_fine)
    d_uk = load(uk, v_uk)
    d_nk = load(nk, v_nk)
    d_fk = load(fk, v_fk)
    d_mf = load(mk.at[:, :, :, pl.ds(0, 128), :], v_mf)
    d_mh = load(mk.at[:, :, :, pl.ds(128, 64), :], v_mh)
    d_bk = load(bk, v_bk)
    d_ck = [load(ck.at[t], v_ck.at[t]) for t in range(3)]

    def arrived(first, last):
        for c, _, cr in copies[first:last]:
            if cr is None:
                c.wait_recv()
            else:
                pl.when(cr)(c.wait_recv)

    v_coarse[:, mine, 128:384] = pack[w]
    cgain, cbias, ubias, mgain, mbias, bbias, nbias, fgain, fbias = [
        v[...].reshape(1, -1) for v in (g_c, b_c, b_u, g_m, b_m, b_b, b_n, g_f, b_f)]
    mbias = mbias + bbias

    xfh[:, 128:256] = jnp.zeros((2560, 128), BF)
    xmh[:, 128:256] = jnp.zeros((864, 128), BF)
    img1[...] = jnp.zeros_like(img1)
    rb_m[...] = jnp.zeros_like(rb_m)
    rb_1[...] = jnp.zeros_like(rb_1)
    img_m[...] = jnp.zeros_like(img_m)

    d_uk.wait()
    fold_weights(v_uk, w4u)
    d_nk.wait()
    fold_weights(v_nk, w4n)
    d_fk.wait()
    pack_fine(v_fk, wfc, wf2)

    def fine_cached(r, beside):
        buf = rb_f.at[r % 2]
        for t in range(2):
            buf[t, 8:88, :] = v_f[t, r].astype(F32)
            if beside:
                buf[t, 7:8, :] = lf[t, r : r + 1, :]
                buf[t, 88:89, :] = rf[t, r : r + 1, :]
        put_cached(xfc, r * 80, 80, buf, 7)

    rb_f[...] = jnp.zeros_like(rb_f)
    xfc[0:80, :] = jnp.zeros((80, 1152), BF)
    xfc[2640:2720, :] = jnp.zeros((80, 1152), BF)
    for i in range(4):
        for r in range(8 * i + 2 if i else 1, min(8 * i + 10, 33)):
            fine_cached(r, False)
        acc_f[i * 640 : i * 640 + 640, :] = nt_dot(taps(xfc, i * 640, 640, 80), wfc[...]) + fbias
    d_mf.wait()
    d_mh.wait()
    d_bk.wait()

    arrived(0, n_fine)
    no_n, no_s, no_w, no_e = a == 0, a == NA - 1, w == 0, w == NW - 1

    @pl.when(no_n)
    def _():
        v_m[:, 0:2] = jnp.zeros((2, 2, 40, 192), BF)
        v_f[:, 0:1] = jnp.zeros((2, 1, 80, 192), BF)

    @pl.when(no_s)
    def _():
        v_m[:, 18:20] = jnp.zeros((2, 2, 40, 192), BF)
        v_f[:, 33:34] = jnp.zeros((2, 1, 80, 192), BF)

    spans = ((0, 64, no_w), (64, 128, no_e), (128, 144, no_n | no_w), (144, 160, no_n | no_e),
             (160, 176, no_s | no_w), (176, 192, no_s | no_e))
    for lo, hi, gone in spans:
        g32[:, lo:hi, :] = jnp.where(gone, 0.0, v_g[:, lo:hi, :].astype(F32))
    for t in range(2):
        for l, m, base, n, s in ((lf, lm, 0, 128, 160), (rf, rm, 64, 144, 176)):
            l[t, 0:1, :] = g32[t, n : n + 1, :]
            l[t, 1:33, :] = g32[t, base : base + 32, :]
            l[t, 33:34, :] = g32[t, s : s + 1, :]
            for c in range(2):
                m[t, c, 0:2, :] = g32[t, n + 1 + 2 * c : n + 3 + 2 * c, :]
                m[t, c, 2:18, :] = g32[t, base + 32 + 16 * c : base + 48 + 16 * c, :]
                m[t, c, 18:20, :] = g32[t, s + 1 + 2 * c : s + 3 + 2 * c, :]

    for r in (0, 33):
        fine_cached(r, True)
    acc_f[0:80, :] += nt_dot(xfc[0:80, :], wfc[:, 0:1152])
    acc_f[2480:2560, :] += nt_dot(xfc[2640:2720, :], wfc[:, 2304:3456])
    own_row = lax.broadcasted_iota(jnp.int32, (40, 1), 0)
    own_row = (own_row >= 1) & (own_row <= 32)
    for l, col, b in ((lf, 0, 0), (rf, 79, 2)):
        beside = jnp.zeros((32, 192), F32)
        for t in range(2):
            v = jnp.where(own_row, l[t], 0.0)
            for ra in range(3):
                beside = beside + nt_dot(v[ra : ra + 32].astype(BF), v_fk[t, ra, b])
        for h in range(32):
            acc_f[h * 80 + col : h * 80 + col + 1, :] += beside[h : h + 1]

    for r in range(20):
        buf = rb_m.at[r % 2]
        for t in range(2):
            buf[t, 8:48, :] = v_m[t, r].astype(F32)
            for c in range(2):
                buf[t, 6 + c : 7 + c, :] = lm[t, c, r : r + 1, :]
                buf[t, 48 + c : 49 + c, :] = rm[t, c, r : r + 1, :]
        put_cached(xmc, r * 48, 48, buf, 6)

    def mid_part(at, n):
        k = jnp.concatenate(
            [v[t, r, b] for r in range(3) for v in (v_mf, v_mh) for t in range(2) for b in range(3)], 0)
        acc_m[at : at + n, :] = jnp.dot(taps(xmc, at, n, 48), k, preferred_element_type=F32) + mbias

    mid_part(0, 864)
    arrived(n_fine, n_main)
    begin(n_far, len(copies))

    arrived(n_main, len(copies))
    for t in range(3):
        d_ck[t].wait()
    lane = lax.broadcasted_iota(jnp.int32, (1, 512), 1)
    keep = jnp.logical_and(jnp.logical_or(lane >= 128, a > 0), jnp.logical_or(lane < 384, a < NA - 1))
    for t in range(3):
        for p in range(4):
            part = jnp.where(keep[:, p * 128 : p * 128 + 128],
                             v_coarse[t, :, p * 128 : p * 128 + 128].astype(F32), 0.0)
            flat = part.T
            if t == 2:
                img_l[p * 4 : p * 4 + 4] = flat.reshape(4, 32, 384)
                flat = act(flat, cgain, 384)
            img_c[p * 4 : p * 4 + 4, 0:32, :] = flat.reshape(4, 32, 384)
        for b in range(3):
            v = img_c[1:15, b : b + 24, :].reshape(336, 384)
            for ra in range(3):
                at = (t * 3 + ra) * 288
                xfc[at : at + 288, b * 384 : b * 384 + 384] = v[ra * 24 : ra * 24 + 288].astype(BF)
    total = img_l[2:14, 1:25, :].reshape(288, 384) + cbias
    for t in range(3):
        x = jnp.concatenate([xfc[(t * 3 + ra) * 288 : (t * 3 + ra + 1) * 288, :] for ra in range(3)], 1)
        k = jnp.concatenate([v_ck[t, ra, b] for ra in range(3) for b in range(3)], 1)
        total = total + nt_dot(x, k)
    rid = lax.broadcasted_iota(jnp.int32, (12, 24, 1), 0) + (a * 8 - 2)
    cid = lax.broadcasted_iota(jnp.int32, (12, 24, 1), 1) + (w * 20 - 2)
    inside = (rid >= 0) & (rid < 128) & (cid >= 0) & (cid < 160)
    img1[:, 0:24, :] = jnp.where(inside, total.reshape(12, 24, 384), 0.0)
    for b in range(2):
        xmc[0:384, b * 384 : b * 384 + 384] = img1[:, b : b + 32, :].reshape(384, 384).astype(BF)

    x = jnp.concatenate([xmc[0:352, 0:768], xmc[32:384, 0:768]], 1)
    u = nt_dot(x, w4u[...])
    for i in range(11):
        put_phases(u[i * 32 : i * 32 + 32, :], ubias, img_m, 2 * i, 5)

    mcol = lax.broadcasted_iota(jnp.int32, (72, 1), 0) + (w * 40 - 8)
    mcol = jnp.where((mcol >= 0) & (mcol < 320), 1.0, 0.0)

    def mid_row(r):
        row = a * 16 - 2 + r
        ok = jnp.where((row >= 0) & (row < 256), 1.0, 0.0)
        buf = rb_1.at[r % 4]
        buf[0:72, :] = act(image_row(img_m, r + 1, slice(0, 72)), mgain, 192) * (mcol * ok)
        put_current(xm2, xmh, r, 18, 48, buf, 6)

    def bypass_row(r):
        xmc[r * 48 : r * 48 + 48, 768:960] = image_row(img_m, r + 2, slice(7, 55)).astype(BF)

    def mid_block(i):
        at = i * 432
        k = jnp.concatenate(
            [p for r in range(3) for p in
             [v_mf[2, r, b] for b in range(3)] + [v_mh[2, r, b] for b in range(2)]]
            + [v_mh[2, r, 2] for r in range(3)] + [jnp.zeros((64, 384), BF)], 0)
        x = jnp.concatenate([taps(xm2, at, 432, 48), xmh[at : at + 432, :]], 1)
        total = (acc_m[at : at + 432, :]
                 + jnp.dot(xmc[at : at + 432, 768:960], v_bk[...], preferred_element_type=F32)
                 + jnp.dot(x, k, preferred_element_type=F32))
        rid = lax.broadcasted_iota(jnp.int32, (9, 48, 1), 0) + (a * 16 - 1 + i * 9)
        cid = lax.broadcasted_iota(jnp.int32, (9, 48, 1), 1) + (w * 40 - 1)
        inside = (rid >= 0) & (rid < 256) & (cid >= 0) & (cid < 320)
        img2[i * 9 : i * 9 + 9, 0:48, :] = jnp.where(inside, total.reshape(9, 48, 384), 0.0)
        for r in range(i * 9, i * 9 + 9):
            for b in range(2):
                xmc[r * 48 : r * 48 + 48, b * 384 : b * 384 + 384] = img2[r, b : b + 48, :].astype(BF)

    def fine_block(first, n):
        at, m = first * 48, n * 48
        x = jnp.concatenate([xmc[at : at + m, 0:768], xmc[at + 48 : at + 48 + m, 0:768]], 1)
        u = nt_dot(x, w4n[...])
        for j in range(n):
            put_phases(u[j * 48 : j * 48 + 48, :], nbias, img_f, 2 * (first + j), 7)

    dones = []
    fcol = lax.broadcasted_iota(jnp.int32, (96, 1), 0) + (w * 80 - 8)
    fcol = jnp.where((fcol >= 0) & (fcol < 640), 1.0, 0.0)

    def fine_rows(first, last):
        for r in range(first, last):
            row = a * 32 - 1 + r
            ok = jnp.where((row >= 0) & (row < 512), 1.0, 0.0)
            buf = rb_1.at[r % 4]
            buf[0:96, :] = act(image_row(img_f, r, slice(0, 96)), fgain, 192) * (fcol * ok)
            put_current(xf2, xfh, r, 32, 80, buf, 7)

    def out_block(i):
        at = i * 640
        total = (image_row(img_f, slice(1 + i * 8, 9 + i * 8), slice(8, 88)).reshape(640, 192)
                 + acc_f[at : at + 640, :] + nt_dot(
                     jnp.concatenate([taps(xf2, at, 640, 80), xfh[at : at + 640, :]], 1), wf2[...]))
        v_f[0, i * 8 : i * 8 + 8] = total.reshape(8, 80, 192).astype(BF)
        rows = pl.ds(i * 8, 8)
        done = pltpu.make_async_copy(v_f.at[0, rows], out.at[rows], osem.at[i])
        done.start()
        dones.append(done)

    for r in range(11):
        mid_row(r)
    for r in range(9):
        bypass_row(r)
    mid_block(0)
    for r in range(11, 20):
        mid_row(r)
    for r in range(9, 18):
        bypass_row(r)
    fine_block(0, 8)
    mid_block(1)
    fine_rows(0, 16)
    fine_block(8, 9)
    out_block(0)
    fine_rows(16, 26)
    out_block(1)
    fine_rows(26, 34)
    out_block(2)
    out_block(3)
    for c, cs, _ in copies:
        if cs is None:
            c.wait_send()
        else:
            pl.when(cs)(c.wait_send)
    for done in dones:
        done.wait()


def call(*args):
    anywhere = pl.BlockSpec(memory_space=pl.ANY)
    vmem = pl.BlockSpec(memory_space=pltpu.VMEM)
    V = pltpu.VMEM
    n = 10 + 7 + 16 + 2
    return pl.pallas_call(
        kernel,
        out_shape=jax.ShapeDtypeStruct((32, 80, 192), BF),
        in_specs=[vmem] * 11 + [anywhere] * 8,
        out_specs=anywhere,
        scratch_shapes=[
            V((3, 384, 512), BF), V((2, 34, 80, 192), BF), V((2, 20, 40, 192), BF), V((2, 192, 192), BF),
            V((3, 3, 3, 384, 384), BF), V((3, 3, 192, 384), BF),
            V((3, 3, 3, 128, 384), BF), V((3, 3, 3, 64, 384), BF),
            V((192, 384), BF), V((3, 3, 192, 384), BF), V((3, 3, 3, 192, 192), BF),
            V((48, 8, 128), F32), V((48, 8, 128), F32), V((2, 192, 192), F32), V((2, 192, 192), BF), V((8, 3, 48, 256), BF),
            V((192, 3456), BF), V((192, 1792), BF), V((768, 1536), BF), V((768, 1536), BF),
            V((2720, 1152), BF), V((2720, 512), BF), V((2560, 256), BF), V((960, 1152), BF), V((960, 512), BF), V((864, 256), BF),
            V((16, 40, 384), F32), V((16, 32, 384), F32), V((12, 40, 384), F32), V((2, 22, 72, 128), F32),
            V((18, 56, 384), F32), V((2, 34, 104, 128), F32), V((2, 2, 96, 192), F32), V((2, 2, 72, 192), F32),
            V((4, 96, 192), F32), V((2, 192, 192), F32),
            V((2, 40, 192), F32), V((2, 40, 192), F32), V((2, 2, 24, 192), F32), V((2, 2, 24, 192), F32),
            V((2560, 192), F32), V((864, 384), F32),
            pltpu.SemaphoreType.DMA((16,)), pltpu.SemaphoreType.DMA((4,)),
            pltpu.SemaphoreType.DMA((n,)), pltpu.SemaphoreType.DMA((n,)),
        ],
        compiler_params=pltpu.CompilerParams(
            collective_id=0, has_side_effects=True, vmem_limit_bytes=63 * 2**20),
    )(*args)


def per_device(
    latent_map, coarse_cache, coarse_gain, coarse_kernel, coarse_bias, upper_kernel, upper_bias,
    middle_cache, middle_gain, middle_kernel, middle_bias, bypass_weight, bypass_bias,
    finer_kernel, finer_bias, fine_cache, fine_gain, fine_kernel, fine_bias,
):
    ft = jnp.transpose(fine_cache, (0, 2, 3, 1))
    mt = jnp.transpose(middle_cache, (0, 2, 3, 1))
    y = call(
        latent_map, coarse_cache, coarse_gain, coarse_bias, upper_bias, middle_gain, middle_bias, bypass_bias,
        finer_bias, fine_gain, fine_bias, ft, mt, coarse_kernel, upper_kernel,
        jnp.transpose(middle_kernel, (0, 1, 2, 4, 3)), bypass_weight.T, finer_kernel, fine_kernel)
    return jnp.transpose(y, (2, 0, 1))


def solution(mesh):
    high = (P("wa", "ha", None), P(None, "wa", "ha", None))
    low = P(None, None, "ha", "wa")
    placed = high + (P(),) * 5 + (low,) + (P(),) * 7 + (low,) + (P(),) * 3
    return jax.shard_map(
        per_device, mesh=mesh, in_specs=placed, out_specs=P(None, "ha", "wa"), check_vma=False
    )
```
